512 devices in a mesh: chan: 128 (over z, y, core), cuts: 4 (over x).
Axes of the slice: x: 4, y: 8, z: 8, core: 2. Of those that a mesh axis runs over, the one named last changes fastest.
Arguments:
- strain: bfloat16 [4, 4096, 8192], P('cuts', 'chan'), may hold values from -6 to 6
- band_taper: float32 [960], replicated, may hold values from 0.5 to 2
- pair_list: int32 [128, 6, 2], P('chan'), may hold values from 0 to 127, as said below
- pair_counts: int32 [128], P('chan'), may hold values from 1 to 6, as said below
Outputs:
- lag_stacks: bfloat16 [2048, 768, 32], P('cuts', 'chan')
The draws below stay inside these ranges and needn't reach their ends.
Inputs may be any that keep to these rules, and one draw needn't show every extreme that they name: `pair_list`: both blocks of every slot of owner b, padded ones too, lie within 8 blocks of b; some owner has a source block exactly 8 above it and some owner a target block exactly 8 below it. `pair_counts`: some owner has 6 live slots and some owner one.
All inputs are finite; a program needn't handle non-finite values.
Results may differ from the reference program's by a relative error of at most 0.0065.
Values may be sent and summed in bfloat16 or wider, within the bound.
A program may use at most 64 MiB of HBM per device.

```python
import math
import jax
import jax.numpy as jnp
from jax import lax

CH_DEV = 32
SAMP = 8192
STRIDE = 4
F0 = 32
NF = 960
SMOOTH = 32
LAG = 1024
PMAX = 6
REACH = 8
CHANNELS = 4096
SLICES = 4
N_CHAN = 128


def pair_layout(key):
    blocks = N_CHAN
    reach = REACH
    width = 2 * reach + 1
    owners = jnp.arange(blocks, dtype=jnp.int32)
    key_order, key_first, key_second, key_count = jax.random.split(key, 4)
    order_keys = jax.random.split(key_order, blocks)
    orders = jax.vmap(lambda sub: jax.random.permutation(sub, width))(order_keys).astype(jnp.int32) - reach
    slot_ids = jnp.arange(PMAX, dtype=jnp.int32)
    src_step = orders[:, slot_ids % width]
    tgt_step = orders[:, (slot_ids + PMAX) % width]
    sources = jnp.clip(owners[:, None] + src_step, 0, blocks - 1)
    targets = jnp.clip(owners[:, None] + tgt_step, 0, blocks - 1)
    first = jax.random.randint(key_first, (), 0, blocks - reach)
    second = jax.random.randint(key_second, (), reach, blocks)
    sources = sources.at[first, 0].set(first + reach)
    targets = targets.at[second, 0].set(second - reach)
    counts = jax.random.randint(key_count, (blocks,), 1, PMAX + 1)
    busiest = jax.random.randint(jax.random.fold_in(key_count, 1), (), 0, blocks)
    lightest = (busiest + 1 + jax.random.randint(jax.random.fold_in(key_count, 2), (), 0, blocks - 1)) % blocks
    counts = counts.at[busiest].set(PMAX).at[lightest].set(1)
    return (jnp.stack([sources, targets], axis=-1).astype(jnp.int32), counts.astype(jnp.int32))


def draw_pair_list(key, part):
    return pair_layout(key)[0]


def draw_pair_counts(key, part):
    return pair_layout(key)[1]


def steps_of(key, shape, pieces, low, high):
    loudness = 1.0
    for position, blocks in pieces:
        heights = jax.random.uniform(jax.random.fold_in(jax.random.fold_in(key, 6), position), (blocks,), jnp.float32, low / len(pieces), high / len(pieces))
        loudness = loudness * jnp.repeat(jnp.exp(heights), shape[position] // blocks).reshape((-1,) + (1,) * (len(shape) - 1 - position))
    return loudness


def normal_values(stream_key, dims, deviation, limit, cuts=(), held_as=jnp.bfloat16):
    drawn = deviation * jax.random.normal(stream_key, dims, jnp.float32)
    if cuts:
        drawn = drawn * steps_of(stream_key, dims, cuts, -0.22, 0.18)
    return jnp.clip(drawn, -limit, limit).astype(held_as)


def setup_inputs(seed: int = 0) -> dict:
    arg_keys = jax.random.split(jax.random.key(seed), 5)
    return {
        "strain": normal_values(arg_keys[0], (SLICES, CHANNELS, SAMP), 1.0, 6.0, ((0, 4), (1, 128))),
        "band_taper": jnp.clip(jnp.exp(jax.random.uniform(arg_keys[1], (NF,), jnp.float32, math.log(0.5), math.log(2.0))), 0.5, 2.0),
        "pair_list": draw_pair_list(jax.random.fold_in(arg_keys[4], 71), 0),
        "pair_counts": draw_pair_counts(jax.random.fold_in(arg_keys[4], 71), 0),
    }


def band_table(offset, length):
    sample_ids = offset + jnp.arange(length, dtype=jnp.int32)
    bin_ids = F0 + jnp.arange(NF, dtype=jnp.int32)
    phases = sample_ids[:, None] * bin_ids[None, :] % SAMP
    angles = phases.astype(jnp.float32) * (2.0 * math.pi / SAMP)
    return jnp.concatenate([jnp.cos(angles), -jnp.sin(angles)], axis=1).astype(jnp.bfloat16)

def spectrum(signal):
    block_len = min(512, SAMP)

    def advance(turn, summed):
        piece = lax.dynamic_slice_in_dim(signal, turn * block_len, block_len, 1)
        return summed + jnp.dot(piece, band_table(turn * block_len, block_len), preferred_element_type=jnp.float32)
    initial = jnp.zeros((signal.shape[0], 2 * NF), jnp.float32)
    return lax.fori_loop(0, SAMP // block_len, advance, initial)

def whiten(spectra, band_taper):
    real_part = spectra[:, :NF]
    imag_part = spectra[:, NF:]
    magnitude = jnp.sqrt(real_part * real_part + imag_part * imag_part)
    bin_ids = jnp.arange(NF, dtype=jnp.int32)
    window = (jnp.abs(bin_ids[:, None] - bin_ids[None, :]) <= SMOOTH).astype(jnp.float32)
    level = jnp.dot(magnitude, window, precision=lax.Precision.HIGHEST) / lax.optimization_barrier(jnp.sum(window, axis=0))
    factor = band_taper / (level + 1e-06)
    return jnp.concatenate([real_part * factor, imag_part * factor], axis=1).astype(jnp.bfloat16)

def cross_spectrum(source, target):
    src_real = source[..., :NF].astype(jnp.float32)
    src_imag = source[..., NF:].astype(jnp.float32)
    tgt_real = target[..., :NF].astype(jnp.float32)
    tgt_imag = target[..., NF:].astype(jnp.float32)
    return jnp.concatenate([src_real * tgt_real + src_imag * tgt_imag, src_imag * tgt_real - src_real * tgt_imag], axis=-1)

def lag_table(lag_begin, lag_count):
    lag_ids = lag_begin + jnp.arange(lag_count, dtype=jnp.int32) - LAG + SAMP
    bin_ids = F0 + jnp.arange(NF, dtype=jnp.int32)
    phases = bin_ids[:, None] * (lag_ids[None, :] * STRIDE) % SAMP
    angles = phases.astype(jnp.float32) * (2.0 * math.pi / SAMP)
    scale = 1.0 / math.sqrt(NF)
    return jnp.concatenate([jnp.cos(angles) * scale, -jnp.sin(angles) * scale], axis=0)

def lag_rows(spectra, lag_begin, lag_count):
    return jnp.einsum('pcf,ft->tpc', spectra, lag_table(lag_begin, lag_count), precision=lax.Precision.HIGHEST)

def reference(strain, band_taper, pair_list, pair_counts):
    slices, channels, samples = strain.shape
    spectra = spectrum(strain.reshape(slices * channels, samples))
    whitened = whiten(spectra, band_taper).reshape(slices, N_CHAN, CH_DEV, 2 * NF)
    live = (jnp.arange(PMAX, dtype=jnp.int32)[None, :] < pair_counts[:, None]).astype(jnp.float32)

    def per_owner(owner_items):
        owner_pairs, owner_live = owner_items
        sources = whitened[:, owner_pairs[:, 0]]
        targets = whitened[:, owner_pairs[:, 1]]
        cross = cross_spectrum(sources, targets) * owner_live[None, :, None, None]
        return lax.optimization_barrier(jnp.sum(cross, axis=0))
    summed = lax.map(per_owner, (pair_list, live))
    flat = summed.reshape(N_CHAN * PMAX, CH_DEV, 2 * NF)
    block_len = min(1024, 2 * LAG)

    def lag_block(turn):
        return lag_rows(flat, turn * block_len, block_len)
    parts = lax.map(lag_block, jnp.arange(2 * LAG // block_len, dtype=jnp.int32))
    return parts.reshape(2 * LAG, N_CHAN * PMAX, CH_DEV).astype(jnp.bfloat16)
```

```python
import math

import jax
import jax.numpy as jnp
import ml_dtypes
import numpy as np
from jax import lax
from jax.experimental import pallas as pl
from jax.experimental.pallas import tpu as pltpu
from jax.sharding import PartitionSpec as P

SAMP = 8192
F0 = 32
NF = 960
SMOOTH = 32
PAIRS = 6
CHAN = 32
SLICES = 4
HOPS = 4
SLOTS = 2 * (2 * HOPS + 1)
MESH = pl.DeviceIdType.MESH
F32 = jnp.float32
BF16 = jnp.bfloat16
ROOT_HALF = math.sqrt(0.5)


def tables():
    n2 = np.arange(1024)
    k2 = np.arange(128)
    angle = 2 * np.pi * ((n2[:, None] * k2[None, :]) % 1024) / 1024
    forward = np.concatenate([np.cos(angle), np.sin(angle)], axis=1).astype(ml_dtypes.bfloat16)
    k1 = np.arange(8)
    angle = 2 * np.pi * k1[:, None] * n2[None, :] / SAMP
    forward_turn = np.concatenate([np.cos(angle), np.sin(angle)], axis=0).astype(np.float32)
    t1 = np.arange(256)
    angle = 2 * np.pi * ((k2[:, None] * t1[None, :]) % 256) / 256
    c, s = np.cos(angle), np.sin(angle)
    lag = np.block([[c, s], [-s, c]]).astype(ml_dtypes.bfloat16)
    angle = 2 * np.pi * k1[:, None] * t1[None, :] / 2048
    gain = ((-1.0) ** k1)[:, None] / math.sqrt(NF)
    turn = np.stack([np.cos(angle) * gain, np.sin(angle) * gain])
    turn = np.repeat(turn.reshape(2, 2, 4, 1, 256), 4, axis=3)
    lag_turn = turn.transpose(0, 2, 1, 3, 4).reshape(2, 4, 8, 256).astype(np.float32)
    bins = np.arange(NF)
    count = np.minimum(bins + SMOOTH, NF - 1) - np.maximum(bins - SMOOTH, 0) + 1
    inverse = np.ones(1024)
    inverse[F0 : F0 + NF] = 1.0 / count
    inverse = inverse.reshape(128, 8).T.astype(np.float32)
    return forward, forward_turn, lag, lag_turn, inverse


def kernel(
    x_ref,
    taper_ref,
    inverse_ref,
    fturn_ref,
    ftab_ref,
    ltab_ref,
    lturn_ref,
    pairs_ref,
    count_ref,
    out_ref,
    y_ref,
    stage0,
    stage1,
    win0,
    win1,
    lhs_ref,
    send0,
    send1,
    land0,
    land1,
    swap_send,
    swap_recv,
    hop_send,
    hop_recv,
    core_send,
    core_recv,
    back_send,
    back_recv,
):
    stage, win, sbuf, land = (stage0, stage1), (win0, win1), (send0, send1), (land0, land1)
    blocks = lax.axis_size("chan")
    me = lax.axis_index("chan")
    cut = lax.axis_index("cuts")
    core = lax.rem(me, 2)
    right = lax.rem(me + 2, blocks)
    left = lax.rem(me + blocks - 2, blocks)
    other = me + 1 - 2 * core

    def at(chan, cuts):
        return {"chan": chan, "cuts": cuts}

    def peer(j):
        return lax.rem(cut + j, SLICES)

    def slot(d):
        return 2 * (d + HOPS) + core

    barrier = pltpu.get_barrier_semaphore()
    for target in [at(right, cut), at(left, cut), at(other, cut)] + [at(me, peer(j)) for j in (1, 2, 3)]:
        pl.semaphore_signal(barrier, inc=1, device_id=target, device_id_type=MESH)

    def butterflies(j, carry):
        o = pl.multiple_of(j * 128, 128)
        x = [x_ref[:, pl.ds(pl.multiple_of(n1 * 1024 + o, 128), 128)].astype(F32) for n1 in range(8)]
        s = [x[n] + x[n + 4] for n in range(4)]
        d = [x[n] - x[n + 4] for n in range(4)]
        e0, e1 = s[0] + s[2], s[1] + s[3]
        dm, dp = (d[1] - d[3]) * ROOT_HALF, (d[1] + d[3]) * ROOT_HALF
        z1 = (d[0] + dm, -(d[2] + dp))
        z3 = (d[0] - dm, d[2] - dp)
        z2 = (s[0] - s[2], s[3] - s[1])
        y_ref[0:32, pl.ds(o, 128)] = (e0 + e1).astype(BF16)
        z = {1: z1, 2: z2, 3: z3, 4: (e0 - e1, None), 5: (z3[0], -z3[1]), 6: (z2[0], -z2[1]), 7: (z1[0], -z1[1])}
        for k1 in range(1, 8):
            c = fturn_ref[k1 : k1 + 1, pl.ds(o, 128)]
            q = fturn_ref[8 + k1 : 9 + k1, pl.ds(o, 128)]
            re, im = z[k1]
            if im is None:
                yr, yi = re * c, -(re * q)
            else:
                yr, yi = re * c + im * q, im * c - re * q
            base = 32 + 64 * (k1 - 1)
            y_ref[base : base + 32, pl.ds(o, 128)] = yr.astype(BF16)
            y_ref[base + 32 : base + 64, pl.ds(o, 128)] = yi.astype(BF16)
        return carry

    lax.fori_loop(0, 8, butterflies, 0)
    r = jnp.dot(y_ref[...], ftab_ref[...], preferred_element_type=F32)
    re = [r[0:32, :128]]
    im = [-r[0:32, 128:]]
    for k1 in range(1, 8):
        base = 32 + 64 * (k1 - 1)
        a, b = r[base : base + 32], r[base + 32 : base + 64]
        re.append(a[:, :128] + b[:, 128:])
        im.append(b[:, :128] - a[:, 128:])

    lane = lax.broadcasted_iota(jnp.int32, (CHAN, 128), 1)
    valid = (lane >= F0 // 8) & (lane < (F0 + NF) // 8)
    mag = [jnp.where(valid, jnp.sqrt(re[k] * re[k] + im[k] * im[k]), 0.0) for k in range(8)]
    low = [mag[0]]
    for k in range(1, 8):
        low.append(low[-1] + mag[k])
    high = [mag[7]]
    for k in range(6, -1, -1):
        high.append(high[-1] + mag[k])
    high = high[::-1]
    total = low[7]
    middle = total
    for step in range(1, 4):
        middle = middle + pltpu.roll(total, step, 1) + pltpu.roll(total, 128 - step, 1)
    upper = lax.broadcasted_iota(jnp.int32, (4, 8, 128), 1) < 4
    for k in range(8):
        level = (middle + pltpu.roll(high[k], 4, 1) + pltpu.roll(low[k], 124, 1)) * inverse_ref[k : k + 1, :]
        factor = taper_ref[k : k + 1, :] / (level + 1e-6)
        re[k] = (re[k] * factor).reshape(4, 8, 128)
        im[k] = (im[k] * factor).reshape(4, 8, 128)
    for k in range(4):
        for h in range(2):
            rows = []
            for part in (re, im):
                a, b = part[k], part[k + 4]
                if h == 0:
                    rows.append(jnp.where(upper, a, pltpu.roll(b, 4, 1)))
                else:
                    rows.append(jnp.where(upper, pltpu.roll(a, 4, 1), b))
            stage[h][:, :, k * 128 : (k + 1) * 128] = jnp.concatenate(rows, axis=1).astype(BF16)

    pl.semaphore_wait(barrier, 6)

    def swap(h, j):
        return pltpu.make_async_remote_copy(
            src_ref=stage[h].at[peer(j)],
            dst_ref=win[h].at[slot(0), cut],
            send_sem=swap_send.at[h, j - 1],
            recv_sem=swap_recv.at[h, j - 1],
            device_id=at(me, peer(j)),
            device_id_type=MESH,
        )

    def hop(h, way, step):
        sign = -1 if way == 0 else 1
        return pltpu.make_async_remote_copy(
            src_ref=win[h].at[slot(sign * (step - 1))],
            dst_ref=win[h].at[slot(sign * step)],
            send_sem=hop_send.at[h, way, step - 1],
            recv_sem=hop_recv.at[h, way, step - 1],
            device_id=at(right if way == 0 else left, cut),
            device_id_type=MESH,
        )

    def across(h, n):
        d = HOPS - 2 * HOPS * core if n == 7 else (0, -1, 1, -2, 2, -3, 3)[n]
        return pltpu.make_async_remote_copy(
            src_ref=win[h].at[slot(d)],
            dst_ref=win[h].at[slot(d)],
            send_sem=core_send.at[h, n],
            recv_sem=core_recv.at[h, n],
            device_id=at(other, cut),
            device_id_type=MESH,
        )

    def back(h, j):
        return pltpu.make_async_remote_copy(
            src_ref=sbuf[h].at[peer(j)],
            dst_ref=land[h].at[cut],
            send_sem=back_send.at[h, j - 1],
            recv_sem=back_recv.at[h, j - 1],
            device_id=at(me, peer(j)),
            device_id_type=MESH,
        )

    sublane = lax.broadcasted_iota(jnp.int32, (1, 8, 1), 1) < 4

    def correlate(h):
        first = me - core

        def pair(p):
            live = jnp.where(p < count_ref[0], 1.0, 0.0).astype(F32)
            a_slot = jnp.clip(pairs_ref[0, p] - first + 2 * HOPS, 0, SLOTS - 1)
            b_slot = jnp.clip(pairs_ref[1, p] - first + 2 * HOPS, 0, SLOTS - 1)
            cr = ci = None
            for s in range(SLICES):
                a = win[h][a_slot, s].astype(F32)
                b = win[h][b_slot, s].astype(F32)
                ar, ai, br, bi = a[:8], a[8:], b[:8], b[8:]
                tr, ti = ar * br + ai * bi, ai * br - ar * bi
                cr, ci = (tr, ti) if cr is None else (cr + tr, ci + ti)
            return cr * live, ci * live

        def two(q, carry):
            cr0, ci0 = pair(2 * q)
            cr1, ci1 = pair(2 * q + 1)
            cr = jnp.concatenate([cr0, cr1], axis=0).astype(BF16)
            ci = jnp.concatenate([ci0, ci1], axis=0).astype(BF16)
            rows = pl.ds(pl.multiple_of(16 * q, 16), 16)
            for k in range(4):
                lhs_ref[k, rows, 0:128] = cr[:, k * 128 : (k + 1) * 128]
                lhs_ref[k, rows, 128:256] = ci[:, k * 128 : (k + 1) * 128]
            return carry

        lax.fori_loop(0, PAIRS // 2, two, 0)
        v = jnp.dot(lhs_ref[...].reshape(4 * 48, 256), ltab_ref[...], preferred_element_type=F32)
        parts = []
        for k in range(4):
            rows = v[48 * k : 48 * (k + 1)].reshape(PAIRS, 8, 512)
            dr, di = rows[:, :, :256], rows[:, :, 256:]
            c, s = lturn_ref[0, k][None], lturn_ref[1, k][None]
            tr, ti = dr * c - di * s, dr * s + di * c
            tr = jnp.where(sublane, tr, -tr) + pltpu.roll(tr, 4, 1)
            ti = jnp.where(sublane, ti, -ti) + pltpu.roll(ti, 4, 1)
            parts.append((tr, ti))
        r0 = parts[0][0]
        c1 = jnp.where(sublane, 1.0, ROOT_HALF)
        c3 = jnp.where(sublane, 1.0, -ROOT_HALF)
        s13 = jnp.where(sublane, 0.0, ROOT_HALF)
        r1, i1 = parts[1][0] * c1 - parts[1][1] * s13, parts[1][0] * s13 + parts[1][1] * c1
        r2 = jnp.where(sublane, parts[2][0], -parts[2][1])
        r3, i3 = parts[3][0] * c3 - parts[3][1] * s13, parts[3][0] * s13 + parts[3][1] * c3
        plus, minus, even, odd = r0 + r2, r0 - r2, r1 + r3, i1 - i3
        for m, value in enumerate((plus + even, minus - odd, plus - even, minus + odd)):
            sbuf[h][m] = value.reshape(48, 256).astype(BF16)
        for j in (1, 2, 3):
            back(h, j).start()
        land[h][cut] = sbuf[h][cut]

    for h in range(2):
        for j in (1, 2, 3):
            swap(h, j).start()
        win[h][slot(0), cut] = stage[h][cut]
    for h in range(2):
        for j in (1, 2, 3):
            swap(h, j).wait_recv()
        hop(h, 0, 1).start()
        hop(h, 1, 1).start()
        across(h, 0).start()
    for step in range(1, HOPS + 1):
        for h in range(2):
            for way in range(2):
                hop(h, way, step).wait_recv()
                if step < HOPS:
                    hop(h, way, step + 1).start()
                    across(h, 2 * step - 1 + way).start()
            if step == HOPS:
                across(h, 7).start()
                for n in range(8):
                    across(h, n).wait_recv()
                correlate(h)

    for h in range(2):
        for j in (1, 2, 3):
            back(h, j).wait_recv()
    top = lax.broadcasted_iota(jnp.int32, (8, 256), 0) < 4
    for p in range(PAIRS):
        for y in range(2):
            halves = []
            for x in (2 * y, 2 * y + 1):
                a = land[0][x, 16 * (p // 2) : 16 * (p // 2) + 16].astype(F32)[8 * (p % 2) : 8 * (p % 2) + 8]
                b = land[1][x, 16 * (p // 2) : 16 * (p // 2) + 16].astype(F32)[8 * (p % 2) : 8 * (p % 2) + 8]
                first = jnp.where(top, a, pltpu.roll(b, 4, 0))
                second = jnp.where(top, pltpu.roll(a, 4, 0), b)
                halves.append(jnp.concatenate([first, second], axis=1))
            base = 32 * p + 16 * y
            out_ref[base : base + 16, :] = jnp.concatenate(halves, axis=0).astype(BF16)

    for h in range(2):
        for j in (1, 2, 3):
            swap(h, j).wait_send()
            back(h, j).wait_send()
        for way in range(2):
            for step in range(1, HOPS + 1):
                hop(h, way, step).wait_send()
        for n in range(8):
            across(h, n).wait_send()


def shards(strain, band_taper, pair_list, pair_counts):
    forward, forward_turn, lag, lag_turn, inverse = (jnp.asarray(t) for t in tables())
    taper = jnp.pad(band_taper, (F0, 1024 - F0 - NF)).reshape(128, 8).T
    pairs = pair_list.transpose(0, 2, 1).reshape(2, PAIRS)
    vmem = pl.BlockSpec(memory_space=pltpu.VMEM)
    smem = pl.BlockSpec(memory_space=pltpu.SMEM)
    dma = pltpu.SemaphoreType.DMA
    window = pltpu.VMEM((SLOTS, SLICES, 16, 512), BF16)
    piece = pltpu.VMEM((SLICES, 16, 512), BF16)
    result = pltpu.VMEM((SLICES, 48, 256), BF16)
    stacks = pl.pallas_call(
        kernel,
        out_shape=jax.ShapeDtypeStruct((PAIRS * CHAN, 512), BF16),
        in_specs=[vmem] * 7 + [smem] * 2,
        out_specs=vmem,
        scratch_shapes=[
            pltpu.VMEM((480, 1024), BF16),
            piece,
            piece,
            window,
            window,
            pltpu.VMEM((4, 48, 256), BF16),
            result,
            result,
            result,
            result,
            dma((2, 3)),
            dma((2, 3)),
            dma((2, 2, HOPS)),
            dma((2, 2, HOPS)),
            dma((2, 8)),
            dma((2, 8)),
            dma((2, 3)),
            dma((2, 3)),
        ],
        compiler_params=pltpu.CompilerParams(
            collective_id=0, has_side_effects=True, vmem_limit_bytes=32 * 1024 * 1024
        ),
    )(strain.reshape(CHAN, SAMP), taper, inverse, forward_turn, forward, lag, lag_turn, pairs, pair_counts)
    return stacks.reshape(PAIRS, CHAN, 512).transpose(2, 0, 1)


def solution(mesh):
    in_specs = (P("cuts", "chan", None), P(), P("chan", None, None), P("chan"))
    out_specs = P("cuts", "chan", None)
    return jax.shard_map(shards, mesh=mesh, in_specs=in_specs, out_specs=out_specs, check_vma=False)
```

```python
import math

import jax
import jax.numpy as jnp
import ml_dtypes
import numpy as np
from jax import lax
from jax.experimental import pallas as pl
from jax.experimental.pallas import tpu as pltpu
from jax.sharding import PartitionSpec as P

SAMP = 8192
F0 = 32
NF = 960
SMOOTH = 32
PAIRS = 6
CHAN = 32
SLICES = 4
HOPS = 4
SLOTS = 2 * (2 * HOPS + 1)
MESH = pl.DeviceIdType.MESH
F32 = jnp.float32
BF16 = jnp.bfloat16
ROOT_HALF = math.sqrt(0.5)


def tables():
    n2 = np.arange(1024)
    k2 = np.arange(128)
    angle = 2 * np.pi * ((n2[:, None] * k2[None, :]) % 1024) / 1024
    forward = np.concatenate([np.cos(angle), np.sin(angle)], axis=1).astype(ml_dtypes.bfloat16)
    k1 = np.arange(8)
    angle = 2 * np.pi * k1[:, None] * n2[None, :] / SAMP
    forward_turn = np.concatenate([np.cos(angle), np.sin(angle)], axis=0).astype(np.float32)
    t1 = np.arange(256)
    angle = 2 * np.pi * ((k2[:, None] * t1[None, :]) % 256) / 256
    c, s = np.cos(angle), np.sin(angle)
    lag = np.block([[c, s], [-s, c]]).astype(ml_dtypes.bfloat16)
    angle = 2 * np.pi * k1[:, None] * t1[None, :] / 2048
    gain = ((-1.0) ** k1)[:, None] / math.sqrt(NF)
    turn = np.stack([np.cos(angle) * gain, np.sin(angle) * gain])
    turn = np.repeat(turn.reshape(2, 2, 4, 1, 256), 4, axis=3)
    lag_turn = turn.transpose(0, 2, 1, 3, 4).reshape(2, 4, 8, 256).astype(np.float32)
    bins = np.arange(NF)
    count = np.minimum(bins + SMOOTH, NF - 1) - np.maximum(bins - SMOOTH, 0) + 1
    inverse = np.ones(1024)
    inverse[F0 : F0 + NF] = 1.0 / count
    inverse = inverse.reshape(128, 8).T.astype(np.float32)
    return forward, forward_turn, lag, lag_turn, inverse


def kernel(
    x_hbm,
    taper_hbm,
    inverse_hbm,
    fturn_hbm,
    ftab_hbm,
    ltab_hbm,
    lturn_hbm,
    pairs_hbm,
    count_hbm,
    out_ref,
    x_ref,
    taper_ref,
    inverse_ref,
    fturn_ref,
    ftab_ref,
    ltab_ref,
    lturn_ref,
    my_pairs,
    my_count,
    its_pairs,
    its_count,
    y_ref,
    stage,
    win0,
    win1,
    win2,
    win3,
    cross_re,
    cross_im,
    lhs_ref,
    sbuf0,
    sbuf1,
    land,
    load_sem,
    list_send,
    list_recv,
    swap_send,
    swap_recv,
    hop_send,
    hop_recv,
    back_send,
    back_recv,
):
    win, sbuf = (win0, win1, win2, win3), (sbuf0, sbuf1)
    blocks = lax.axis_size("chan")
    me = lax.axis_index("chan")
    cut = lax.axis_index("cuts")
    core = lax.rem(me, 2)
    right = lax.rem(me + 2, blocks)
    left = lax.rem(me + blocks - 2, blocks)
    other = me + 1 - 2 * core

    def at(chan, cuts):
        return {"chan": chan, "cuts": cuts}

    def peer(i):
        return lax.rem(cut + i, SLICES)

    group = [(i, r) for i in range(SLICES) for r in range(2) if (i, r) != (0, 0)]

    def member(i, r):
        return at(other if r else me, peer(i))

    barrier = pltpu.get_barrier_semaphore()
    for target in [at(right, cut), at(left, cut)] + [member(i, r) for i, r in group]:
        pl.semaphore_signal(barrier, inc=1, device_id=target, device_id_type=MESH)

    loads = []
    for n, (src, dst) in enumerate(
        [
            (x_hbm, x_ref),
            (fturn_hbm, fturn_ref),
            (ftab_hbm, ftab_ref),
            (taper_hbm, taper_ref),
            (inverse_hbm, inverse_ref),
            (ltab_hbm, ltab_ref),
            (lturn_hbm, lturn_ref),
            (pairs_hbm, my_pairs),
            (count_hbm, my_count),
        ]
    ):
        loads.append(pltpu.make_async_copy(src, dst, load_sem.at[n]))
        loads[-1].start()

    def taper_rows():
        row = lax.broadcasted_iota(jnp.int32, (8, NF), 0)
        bins = lax.broadcasted_iota(jnp.int32, (8, NF), 1)
        rest = jnp.where(lax.rem(bins, 8) == row, jnp.broadcast_to(taper_ref[...], (8, NF)), 0.0)
        terms = []
        for _ in range(3):
            term = rest.astype(BF16)
            rest = rest - term.astype(F32)
            terms.append(term.astype(F32))
        terms.append(jnp.zeros_like(rest))
        bins = lax.broadcasted_iota(jnp.int32, (NF, 128), 0)
        lanes = lax.broadcasted_iota(jnp.int32, (NF, 128), 1)
        pick = jnp.where(bins // 8 == lanes - F0 // 8, 1.0, 0.0).astype(BF16)
        g = jnp.dot(jnp.concatenate(terms, axis=0).astype(BF16), pick, preferred_element_type=F32)
        return g[0:8] + g[8:16] + g[16:24]

    loads[3].wait()
    taper = taper_rows()

    def butterflies(j, carry):
        o = pl.multiple_of(j * 128, 128)
        x = [x_ref[:, pl.ds(pl.multiple_of(n1 * 1024 + o, 128), 128)].astype(F32) for n1 in range(8)]
        s = [x[n] + x[n + 4] for n in range(4)]
        d = [x[n] - x[n + 4] for n in range(4)]
        e0, e1 = s[0] + s[2], s[1] + s[3]
        dm, dp = (d[1] - d[3]) * ROOT_HALF, (d[1] + d[3]) * ROOT_HALF
        z1 = (d[0] + dm, -(d[2] + dp))
        z3 = (d[0] - dm, d[2] - dp)
        z2 = (s[0] - s[2], s[3] - s[1])
        y_ref[0:32, pl.ds(o, 128)] = (e0 + e1).astype(BF16)
        z = {1: z1, 2: z2, 3: z3, 4: (e0 - e1, None), 5: (z3[0], -z3[1]), 6: (z2[0], -z2[1]), 7: (z1[0], -z1[1])}
        for k1 in range(1, 8):
            c = fturn_ref[k1 : k1 + 1, pl.ds(o, 128)]
            q = fturn_ref[8 + k1 : 9 + k1, pl.ds(o, 128)]
            re, im = z[k1]
            if im is None:
                yr, yi = re * c, -(re * q)
            else:
                yr, yi = re * c + im * q, im * c - re * q
            base = 32 + 64 * (k1 - 1)
            y_ref[base : base + 32, pl.ds(o, 128)] = yr.astype(BF16)
            y_ref[base + 32 : base + 64, pl.ds(o, 128)] = yi.astype(BF16)
        return carry

    loads[0].wait()
    loads[1].wait()
    lax.fori_loop(0, 8, butterflies, 0)
    loads[2].wait()
    r = jnp.dot(y_ref[...], ftab_ref[...], preferred_element_type=F32)
    re = [r[0:32, :128]]
    im = [-r[0:32, 128:]]
    for k1 in range(1, 8):
        base = 32 + 64 * (k1 - 1)
        a, b = r[base : base + 32], r[base + 32 : base + 64]
        re.append(a[:, :128] + b[:, 128:])
        im.append(b[:, :128] - a[:, 128:])

    loads[4].wait()
    lane = lax.broadcasted_iota(jnp.int32, (CHAN, 128), 1)
    valid = (lane >= F0 // 8) & (lane < (F0 + NF) // 8)
    mag = [jnp.where(valid, jnp.sqrt(re[k] * re[k] + im[k] * im[k]), 0.0) for k in range(8)]
    low = [mag[0]]
    for k in range(1, 8):
        low.append(low[-1] + mag[k])
    high = [mag[7]]
    for k in range(6, -1, -1):
        high.append(high[-1] + mag[k])
    high = high[::-1]
    total = low[7]
    middle = total
    for step in range(1, 4):
        middle = middle + pltpu.roll(total, step, 1) + pltpu.roll(total, 128 - step, 1)
    upper = lax.broadcasted_iota(jnp.int32, (4, 8, 128), 1) < 4
    for k in range(8):
        level = (middle + pltpu.roll(high[k], 4, 1) + pltpu.roll(low[k], 124, 1)) * inverse_ref[k : k + 1, :]
        factor = taper[k : k + 1, :] / (level + 1e-6)
        re[k] = (re[k] * factor).reshape(4, 8, 128)
        im[k] = (im[k] * factor).reshape(4, 8, 128)
    for k in range(4):
        for h in range(2):
            rows = []
            for part in (re, im):
                a, b = part[k], part[k + 4]
                if h == 0:
                    rows.append(jnp.where(upper, a, pltpu.roll(b, 4, 1)))
                else:
                    rows.append(jnp.where(upper, pltpu.roll(a, 4, 1), b))
            stage[h, :, :, k * 128 : (k + 1) * 128] = jnp.concatenate(rows, axis=1).astype(BF16)

    pl.semaphore_wait(barrier, 9)

    def swap(i, r):
        return pltpu.make_async_remote_copy(
            src_ref=stage.at[1 - core if r else core, peer(i)],
            dst_ref=win[(SLICES - i) % SLICES].at[HOPS, core],
            send_sem=swap_send.at[i, r],
            recv_sem=swap_recv.at[i, r],
            device_id=member(i, r),
            device_id_type=MESH,
        )

    def hop(j, way, step):
        sign = -1 if way == 0 else 1
        return pltpu.make_async_remote_copy(
            src_ref=win[j].at[HOPS + sign * (step - 1)],
            dst_ref=win[j].at[HOPS + sign * step],
            send_sem=hop_send.at[j, way, step - 1],
            recv_sem=hop_recv.at[j, way, step - 1],
            device_id=at(right if way == 0 else left, cut),
            device_id_type=MESH,
        )

    def back(i, r):
        return pltpu.make_async_remote_copy(
            src_ref=sbuf[r].at[peer(i)],
            dst_ref=land.at[core, cut],
            send_sem=back_send.at[i, r],
            recv_sem=back_recv.at[i, r],
            device_id=member(i, r),
            device_id_type=MESH,
        )

    def lists(n):
        src, dst = ((pairs_hbm, its_pairs), (count_hbm, its_count))[n]
        return pltpu.make_async_remote_copy(
            src_ref=src,
            dst_ref=dst,
            send_sem=list_send.at[n],
            recv_sem=list_recv.at[n],
            device_id=at(other, cut),
            device_id_type=MESH,
        )

    order = (0, 1, 3, 2)
    swap(0, 1).start()
    for i in (3, 1, 2):
        for r in range(2):
            swap(i, r).start()
    win[0][HOPS, core] = stage[core, cut]
    for n in range(2):
        lists(n).start()
    for n in (5, 6, 7, 8):
        loads[n].wait()

    def add_slice(j, fresh):
        first = me - core

        def pair(p, carry):
            for r, pairs in ((0, my_pairs), (1, its_pairs)):
                a_slot = jnp.clip(pairs[0, p] - first + 2 * HOPS, 0, SLOTS - 1)
                b_slot = jnp.clip(pairs[1, p] - first + 2 * HOPS, 0, SLOTS - 1)
                a = win[j][a_slot // 2, lax.rem(a_slot, 2)].astype(F32)
                b = win[j][b_slot // 2, lax.rem(b_slot, 2)].astype(F32)
                ar, ai, br, bi = a[:8], a[8:], b[:8], b[8:]
                tr, ti = ar * br + ai * bi, ai * br - ar * bi
                if not fresh:
                    tr, ti = tr + cross_re[r, p], ti + cross_im[r, p]
                cross_re[r, p] = tr
                cross_im[r, p] = ti
            return carry

        lax.fori_loop(0, PAIRS, pair, 0)

    sublane = lax.broadcasted_iota(jnp.int32, (1, 8, 1), 1) < 4

    def correlate(r, count_ref):
        live = [jnp.where(p < count_ref[0], 1.0, 0.0).astype(F32) for p in range(PAIRS)]
        for q in range(PAIRS // 2):
            cr = jnp.concatenate([cross_re[r, 2 * q + e] * live[2 * q + e] for e in range(2)], axis=0).astype(BF16)
            ci = jnp.concatenate([cross_im[r, 2 * q + e] * live[2 * q + e] for e in range(2)], axis=0).astype(BF16)
            for k in range(4):
                lhs_ref[r, k, 16 * q : 16 * q + 16, 0:128] = cr[:, k * 128 : (k + 1) * 128]
                lhs_ref[r, k, 16 * q : 16 * q + 16, 128:256] = ci[:, k * 128 : (k + 1) * 128]
        v = jnp.dot(lhs_ref[r].reshape(4 * 48, 256), ltab_ref[...], preferred_element_type=F32)
        parts = []
        for k in range(4):
            rows = v[48 * k : 48 * (k + 1)].reshape(PAIRS, 8, 512)
            dr, di = rows[:, :, :256], rows[:, :, 256:]
            c, s = lturn_ref[0, k][None], lturn_ref[1, k][None]
            tr, ti = dr * c - di * s, dr * s + di * c
            tr = jnp.where(sublane, tr, -tr) + pltpu.roll(tr, 4, 1)
            ti = jnp.where(sublane, ti, -ti) + pltpu.roll(ti, 4, 1)
            parts.append((tr, ti))
        r0 = parts[0][0]
        c1 = jnp.where(sublane, 1.0, ROOT_HALF)
        c3 = jnp.where(sublane, 1.0, -ROOT_HALF)
        s13 = jnp.where(sublane, 0.0, ROOT_HALF)
        r1, i1 = parts[1][0] * c1 - parts[1][1] * s13, parts[1][0] * s13 + parts[1][1] * c1
        r2 = jnp.where(sublane, parts[2][0], -parts[2][1])
        r3, i3 = parts[3][0] * c3 - parts[3][1] * s13, parts[3][0] * s13 + parts[3][1] * c3
        plus, minus, even, odd = r0 + r2, r0 - r2, r1 + r3, i1 - i3
        for m, value in enumerate((plus + even, minus - odd, plus - even, minus + odd)):
            sbuf[r][m] = value.reshape(48, 256).astype(BF16)

    for j in order:
        if j == 0:
            swap(0, 1).wait_recv()
        else:
            swap(SLICES - j, 0).wait_recv()
            swap(SLICES - j, 1).wait_recv()
        hop(j, 0, 1).start()
        hop(j, 1, 1).start()
    for n in range(2):
        lists(n).wait_recv()
    for step in range(1, HOPS + 1):
        for j in order:
            for way in range(2):
                hop(j, way, step).wait_recv()
                if step < HOPS:
                    hop(j, way, step + 1).start()
            if step == HOPS:
                add_slice(j, j == order[0])
    correlate(1, its_count)
    for i in (2, 1, 3, 0):
        back(i, 1).start()
    correlate(0, my_count)
    for i in (2, 1, 3):
        back(i, 0).start()
    land[core, cut] = sbuf[0][cut]

    for i, r in group:
        back(i, r).wait_recv()
    top = lax.broadcasted_iota(jnp.int32, (8, 256), 0) < 4
    for p in range(PAIRS):
        for y in range(2):
            halves = []
            for x in (2 * y, 2 * y + 1):
                a = land[0, x, 16 * (p // 2) : 16 * (p // 2) + 16].astype(F32)[8 * (p % 2) : 8 * (p % 2) + 8]
                b = land[1, x, 16 * (p // 2) : 16 * (p // 2) + 16].astype(F32)[8 * (p % 2) : 8 * (p % 2) + 8]
                first = jnp.where(top, a, pltpu.roll(b, 4, 0))
                second = jnp.where(top, pltpu.roll(a, 4, 0), b)
                halves.append(jnp.concatenate([first, second], axis=1))
            base = 32 * p + 16 * y
            out_ref[base : base + 16, :] = jnp.concatenate(halves, axis=0).astype(BF16)

    for n in range(2):
        lists(n).wait_send()
    for i, r in group:
        swap(i, r).wait_send()
        back(i, r).wait_send()
    for j in range(SLICES):
        for way in range(2):
            for step in range(1, HOPS + 1):
                hop(j, way, step).wait_send()


def shards(strain, band_taper, pair_list, pair_counts):
    forward, forward_turn, lag, lag_turn, inverse = (jnp.asarray(t) for t in tables())
    pairs = pair_list.transpose(0, 2, 1).reshape(2, PAIRS)
    operands = (
        strain.reshape(CHAN, SAMP),
        band_taper.reshape(1, NF),
        inverse,
        forward_turn,
        forward,
        lag,
        lag_turn,
        pairs,
        pair_counts,
    )
    dma = pltpu.SemaphoreType.DMA
    window = pltpu.VMEM((2 * HOPS + 1, 2, 16, 512), BF16)
    result = pltpu.VMEM((SLICES, 48, 256), BF16)
    stacks = pl.pallas_call(
        kernel,
        out_shape=jax.ShapeDtypeStruct((PAIRS * CHAN, 512), BF16),
        in_specs=[pl.BlockSpec(memory_space=pl.ANY)] * len(operands),
        out_specs=pl.BlockSpec(memory_space=pltpu.VMEM),
        scratch_shapes=[pltpu.VMEM(v.shape, v.dtype) for v in operands[:7]]
        + [
            pltpu.SMEM((2, PAIRS), jnp.int32),
            pltpu.SMEM((1,), jnp.int32),
            pltpu.SMEM((2, PAIRS), jnp.int32),
            pltpu.SMEM((1,), jnp.int32),
            pltpu.VMEM((480, 1024), BF16),
            pltpu.VMEM((2, SLICES, 16, 512), BF16),
            window,
            window,
            window,
            window,
            pltpu.VMEM((2, PAIRS, 8, 512), F32),
            pltpu.VMEM((2, PAIRS, 8, 512), F32),
            pltpu.VMEM((2, 4, 48, 256), BF16),
            result,
            result,
            pltpu.VMEM((2, SLICES, 48, 256), BF16),
            dma((len(operands),)),
            dma((2,)),
            dma((2,)),
            dma((SLICES, 2)),
            dma((SLICES, 2)),
            dma((SLICES, 2, HOPS)),
            dma((SLICES, 2, HOPS)),
            dma((SLICES, 2)),
            dma((SLICES, 2)),
        ],
        compiler_params=pltpu.CompilerParams(
            collective_id=0, has_side_effects=True, vmem_limit_bytes=60 * 1024 * 1024
        ),
    )(*operands)
    return stacks.reshape(PAIRS, CHAN, 512).transpose(2, 0, 1)


def solution(mesh):
    in_specs = (P("cuts", "chan", None), P(), P("chan", None, None), P("chan"))
    out_specs = P("cuts", "chan", None)
    return jax.shard_map(shards, mesh=mesh, in_specs=in_specs, out_specs=out_specs, check_vma=False)
```

```python
import math

import jax
import jax.numpy as jnp
import ml_dtypes
import numpy as np
from jax import lax
from jax.experimental import pallas as pl
from jax.experimental.pallas import tpu as pltpu
from jax.sharding import PartitionSpec as P

SAMP = 8192
F0 = 32
NF = 960
SMOOTH = 32
PAIRS = 6
CHAN = 32
SLICES = 4
HOPS = 4
SLOTS = 2 * (2 * HOPS + 1)
MESH = pl.DeviceIdType.MESH
F32 = jnp.float32
BF16 = jnp.bfloat16
ROOT_HALF = math.sqrt(0.5)


def tables():
    n2 = np.arange(1024)
    k2 = np.arange(128)
    angle = 2 * np.pi * ((n2[:, None] * k2[None, :]) % 1024) / 1024
    forward = np.concatenate([np.cos(angle), np.sin(angle)], axis=1).astype(ml_dtypes.bfloat16)
    k1 = np.arange(8)
    angle = 2 * np.pi * k1[:, None] * n2[None, :] / SAMP
    forward_turn = np.concatenate([np.cos(angle), np.sin(angle)], axis=0).astype(np.float32)
    t1 = np.arange(256)
    angle = 2 * np.pi * ((k2[:, None] * t1[None, :]) % 256) / 256
    c, s = np.cos(angle), np.sin(angle)
    lag = np.block([[c, s], [-s, c]]).astype(ml_dtypes.bfloat16)
    angle = 2 * np.pi * k1[:, None] * t1[None, :] / 2048
    gain = ((-1.0) ** k1)[:, None] / math.sqrt(NF)
    turn = np.stack([np.cos(angle) * gain, np.sin(angle) * gain])
    turn = np.repeat(turn.reshape(2, 2, 4, 1, 256), 4, axis=3)
    lag_turn = turn.transpose(0, 2, 1, 3, 4).reshape(2, 4, 8, 256).astype(np.float32)
    bins = np.arange(NF)
    count = np.minimum(bins + SMOOTH, NF - 1) - np.maximum(bins - SMOOTH, 0) + 1
    inverse = np.ones(1024)
    inverse[F0 : F0 + NF] = 1.0 / count
    inverse = inverse.reshape(128, 8).T.astype(np.float32)
    return forward, forward_turn, lag, lag_turn, inverse


def kernel(
    x_hbm,
    taper_hbm,
    inverse_hbm,
    fturn_hbm,
    ftab_hbm,
    ltab_hbm,
    lturn_hbm,
    pairs_hbm,
    count_hbm,
    out_ref,
    x_ref,
    taper_ref,
    inverse_ref,
    fturn_ref,
    ftab_ref,
    ltab_ref,
    lturn_ref,
    my_pairs,
    my_count,
    its_pairs,
    its_count,
    y_ref,
    stage,
    win0,
    win1,
    win2,
    win3,
    cross_re,
    cross_im,
    lhs_ref,
    sbuf0,
    sbuf1,
    land,
    load_sem,
    list_send,
    list_recv,
    swap_send,
    swap_recv,
    hop_send,
    hop_recv,
    back_send,
    back_recv,
):
    win, sbuf = (win0, win1, win2, win3), (sbuf0, sbuf1)
    blocks = lax.axis_size("chan")
    me = lax.axis_index("chan")
    cut = lax.axis_index("cuts")
    core = lax.rem(me, 2)
    chip = me // 2
    chips = blocks // 2
    other = me + 1 - 2 * core

    def at(chan, cuts):
        return {"chan": chan, "cuts": cuts}

    def peer(i):
        return lax.rem(cut + i, SLICES)

    group = [(i, r) for i in range(SLICES) for r in range(2) if (i, r) != (0, 0)]

    def member(i, r):
        return at(other if r else me, peer(i))

    barrier = pltpu.get_barrier_semaphore()
    for i, r in group:
        pl.semaphore_signal(barrier, inc=1, device_id=member(i, r), device_id_type=MESH)

    @pl.when(chip + 1 < chips)
    def _():
        pl.semaphore_signal(barrier, inc=1, device_id=at(me + 2, cut), device_id_type=MESH)

    @pl.when(chip >= 1)
    def _():
        pl.semaphore_signal(barrier, inc=1, device_id=at(me - 2, cut), device_id_type=MESH)

    loads = []
    for n, (src, dst) in enumerate(
        [
            (x_hbm, x_ref),
            (fturn_hbm, fturn_ref),
            (ftab_hbm, ftab_ref),
            (taper_hbm, taper_ref),
            (inverse_hbm, inverse_ref),
            (ltab_hbm, ltab_ref),
            (lturn_hbm, lturn_ref),
            (pairs_hbm, my_pairs),
            (count_hbm, my_count),
        ]
    ):
        loads.append(pltpu.make_async_copy(src, dst, load_sem.at[n]))
        loads[-1].start()

    def taper_rows():
        row = lax.broadcasted_iota(jnp.int32, (8, NF), 0)
        bins = lax.broadcasted_iota(jnp.int32, (8, NF), 1)
        rest = jnp.where(lax.rem(bins, 8) == row, jnp.broadcast_to(taper_ref[...], (8, NF)), 0.0)
        terms = []
        for _ in range(3):
            term = rest.astype(BF16)
            rest = rest - term.astype(F32)
            terms.append(term.astype(F32))
        terms.append(jnp.zeros_like(rest))
        bins = lax.broadcasted_iota(jnp.int32, (NF, 128), 0)
        lanes = lax.broadcasted_iota(jnp.int32, (NF, 128), 1)
        pick = jnp.where(bins // 8 == lanes - F0 // 8, 1.0, 0.0).astype(BF16)
        g = jnp.dot(jnp.concatenate(terms, axis=0).astype(BF16), pick, preferred_element_type=F32)
        return g[0:8] + g[8:16] + g[16:24]

    loads[3].wait()
    taper = taper_rows()

    def butterflies(j, carry):
        o = pl.multiple_of(j * 128, 128)
        x = [x_ref[:, pl.ds(pl.multiple_of(n1 * 1024 + o, 128), 128)].astype(F32) for n1 in range(8)]
        s = [x[n] + x[n + 4] for n in range(4)]
        d = [x[n] - x[n + 4] for n in range(4)]
        e0, e1 = s[0] + s[2], s[1] + s[3]
        dm, dp = (d[1] - d[3]) * ROOT_HALF, (d[1] + d[3]) * ROOT_HALF
        z1 = (d[0] + dm, -(d[2] + dp))
        z3 = (d[0] - dm, d[2] - dp)
        z2 = (s[0] - s[2], s[3] - s[1])
        y_ref[0:32, pl.ds(o, 128)] = (e0 + e1).astype(BF16)
        z = {1: z1, 2: z2, 3: z3, 4: (e0 - e1, None), 5: (z3[0], -z3[1]), 6: (z2[0], -z2[1]), 7: (z1[0], -z1[1])}
        for k1 in range(1, 8):
            c = fturn_ref[k1 : k1 + 1, pl.ds(o, 128)]
            q = fturn_ref[8 + k1 : 9 + k1, pl.ds(o, 128)]
            re, im = z[k1]
            if im is None:
                yr, yi = re * c, -(re * q)
            else:
                yr, yi = re * c + im * q, im * c - re * q
            base = 32 + 64 * (k1 - 1)
            y_ref[base : base + 32, pl.ds(o, 128)] = yr.astype(BF16)
            y_ref[base + 32 : base + 64, pl.ds(o, 128)] = yi.astype(BF16)
        return carry

    loads[0].wait()
    loads[1].wait()
    lax.fori_loop(0, 8, butterflies, 0)
    loads[2].wait()
    r = jnp.dot(y_ref[...], ftab_ref[...], preferred_element_type=F32)
    re = [r[0:32, :128]]
    im = [-r[0:32, 128:]]
    for k1 in range(1, 8):
        base = 32 + 64 * (k1 - 1)
        a, b = r[base : base + 32], r[base + 32 : base + 64]
        re.append(a[:, :128] + b[:, 128:])
        im.append(b[:, :128] - a[:, 128:])

    loads[4].wait()
    lane = lax.broadcasted_iota(jnp.int32, (CHAN, 128), 1)
    valid = (lane >= F0 // 8) & (lane < (F0 + NF) // 8)
    mag = [jnp.where(valid, jnp.sqrt(re[k] * re[k] + im[k] * im[k]), 0.0) for k in range(8)]
    low = [mag[0]]
    for k in range(1, 8):
        low.append(low[-1] + mag[k])
    high = [mag[7]]
    for k in range(6, -1, -1):
        high.append(high[-1] + mag[k])
    high = high[::-1]
    total = low[7]
    middle = total
    for step in range(1, 4):
        middle = middle + pltpu.roll(total, step, 1) + pltpu.roll(total, 128 - step, 1)
    upper = lax.broadcasted_iota(jnp.int32, (4, 8, 128), 1) < 4
    for k in range(8):
        level = (middle + pltpu.roll(high[k], 4, 1) + pltpu.roll(low[k], 124, 1)) * inverse_ref[k : k + 1, :]
        factor = taper[k : k + 1, :] / (level + 1e-6)
        re[k] = (re[k] * factor).reshape(4, 8, 128)
        im[k] = (im[k] * factor).reshape(4, 8, 128)
    for k in range(4):
        for h in range(2):
            rows = []
            for part in (re, im):
                a, b = part[k], part[k + 4]
                if h == 0:
                    rows.append(jnp.where(upper, a, pltpu.roll(b, 4, 1)))
                else:
                    rows.append(jnp.where(upper, pltpu.roll(a, 4, 1), b))
            stage[h, :, :, k * 128 : (k + 1) * 128] = jnp.concatenate(rows, axis=1).astype(BF16)

    pl.semaphore_wait(barrier, 7 + jnp.where(chip + 1 < chips, 1, 0) + jnp.where(chip >= 1, 1, 0))

    def swap(i, r):
        return pltpu.make_async_remote_copy(
            src_ref=stage.at[1 - core if r else core, peer(i)],
            dst_ref=win[(SLICES - i) % SLICES].at[HOPS, core],
            send_sem=swap_send.at[i, r],
            recv_sem=swap_recv.at[i, r],
            device_id=member(i, r),
            device_id_type=MESH,
        )

    def hop(j, way, step):
        sign = -1 if way == 0 else 1
        return pltpu.make_async_remote_copy(
            src_ref=win[j].at[HOPS + sign * (step - 1)],
            dst_ref=win[j].at[HOPS + sign * step],
            send_sem=hop_send.at[j, way, step - 1],
            recv_sem=hop_recv.at[j, way, step - 1],
            device_id=at(me - 2 * sign, cut),
            device_id_type=MESH,
        )

    def send_hop(j, way, step):
        here = chip >= step - 1 if way == 0 else chip + step - 1 < chips
        there = chip + 1 < chips if way == 0 else chip >= 1

        @pl.when(here & there)
        def _():
            hop(j, way, step).start()

    def end_hop(j, way, step):
        here = chip >= step - 1 if way == 0 else chip + step - 1 < chips
        there = chip + 1 < chips if way == 0 else chip >= 1

        @pl.when(here & there)
        def _():
            hop(j, way, step).wait_send()

    def take_hop(j, way, step):
        @pl.when(chip >= step if way == 0 else chip + step < chips)
        def _():
            hop(j, way, step).wait_recv()

    def back(i, r):
        return pltpu.make_async_remote_copy(
            src_ref=sbuf[r].at[peer(i)],
            dst_ref=land.at[core, cut],
            send_sem=back_send.at[i, r],
            recv_sem=back_recv.at[i, r],
            device_id=member(i, r),
            device_id_type=MESH,
        )

    def lists(n):
        src, dst = ((pairs_hbm, its_pairs), (count_hbm, its_count))[n]
        return pltpu.make_async_remote_copy(
            src_ref=src,
            dst_ref=dst,
            send_sem=list_send.at[n],
            recv_sem=list_recv.at[n],
            device_id=at(other, cut),
            device_id_type=MESH,
        )

    order = (0, 1, 3, 2)
    swap(0, 1).start()
    for i in (3, 1, 2):
        for r in range(2):
            swap(i, r).start()
    win[0][HOPS, core] = stage[core, cut]
    for n in range(2):
        lists(n).start()
    for n in (5, 6, 7, 8):
        loads[n].wait()

    def add_slice(j, fresh):
        first = me - core

        def pair(p, carry):
            for r, pairs in ((0, my_pairs), (1, its_pairs)):
                a_slot = jnp.clip(pairs[0, p] - first + 2 * HOPS, 0, SLOTS - 1)
                b_slot = jnp.clip(pairs[1, p] - first + 2 * HOPS, 0, SLOTS - 1)
                a = win[j][a_slot // 2, lax.rem(a_slot, 2)].astype(F32)
                b = win[j][b_slot // 2, lax.rem(b_slot, 2)].astype(F32)
                ar, ai, br, bi = a[:8], a[8:], b[:8], b[8:]
                tr, ti = ar * br + ai * bi, ai * br - ar * bi
                if not fresh:
                    tr, ti = tr + cross_re[r, p], ti + cross_im[r, p]
                cross_re[r, p] = tr
                cross_im[r, p] = ti
            return carry

        lax.fori_loop(0, PAIRS, pair, 0)

    sublane = lax.broadcasted_iota(jnp.int32, (1, 8, 1), 1) < 4

    def correlate(r, count_ref):
        live = [jnp.where(p < count_ref[0], 1.0, 0.0).astype(F32) for p in range(PAIRS)]
        for q in range(PAIRS // 2):
            cr = jnp.concatenate([cross_re[r, 2 * q + e] * live[2 * q + e] for e in range(2)], axis=0).astype(BF16)
            ci = jnp.concatenate([cross_im[r, 2 * q + e] * live[2 * q + e] for e in range(2)], axis=0).astype(BF16)
            for k in range(4):
                lhs_ref[r, k, 16 * q : 16 * q + 16, 0:128] = cr[:, k * 128 : (k + 1) * 128]
                lhs_ref[r, k, 16 * q : 16 * q + 16, 128:256] = ci[:, k * 128 : (k + 1) * 128]
        v = jnp.dot(lhs_ref[r].reshape(4 * 48, 256), ltab_ref[...], preferred_element_type=F32)
        parts = []
        for k in range(4):
            rows = v[48 * k : 48 * (k + 1)].reshape(PAIRS, 8, 512)
            dr, di = rows[:, :, :256], rows[:, :, 256:]
            c, s = lturn_ref[0, k][None], lturn_ref[1, k][None]
            tr, ti = dr * c - di * s, dr * s + di * c
            tr = jnp.where(sublane, tr, -tr) + pltpu.roll(tr, 4, 1)
            ti = jnp.where(sublane, ti, -ti) + pltpu.roll(ti, 4, 1)
            parts.append((tr, ti))
        r0 = parts[0][0]
        c1 = jnp.where(sublane, 1.0, ROOT_HALF)
        c3 = jnp.where(sublane, 1.0, -ROOT_HALF)
        s13 = jnp.where(sublane, 0.0, ROOT_HALF)
        r1, i1 = parts[1][0] * c1 - parts[1][1] * s13, parts[1][0] * s13 + parts[1][1] * c1
        r2 = jnp.where(sublane, parts[2][0], -parts[2][1])
        r3, i3 = parts[3][0] * c3 - parts[3][1] * s13, parts[3][0] * s13 + parts[3][1] * c3
        plus, minus, even, odd = r0 + r2, r0 - r2, r1 + r3, i1 - i3
        for m, value in enumerate((plus + even, minus - odd, plus - even, minus + odd)):
            sbuf[r][m] = value.reshape(48, 256).astype(BF16)

    for j in order:
        if j == 0:
            swap(0, 1).wait_recv()
        else:
            swap(SLICES - j, 0).wait_recv()
            swap(SLICES - j, 1).wait_recv()
        send_hop(j, 0, 1)
        send_hop(j, 1, 1)
    for n in range(2):
        lists(n).wait_recv()
    for step in range(1, HOPS + 1):
        for j in order:
            for way in range(2):
                take_hop(j, way, step)
                if step < HOPS:
                    send_hop(j, way, step + 1)
            if step == HOPS:
                add_slice(j, j == order[0])
    correlate(1, its_count)
    for i in (2, 1, 3, 0):
        back(i, 1).start()
    correlate(0, my_count)
    for i in (2, 1, 3):
        back(i, 0).start()
    land[core, cut] = sbuf[0][cut]

    for i, r in group:
        back(i, r).wait_recv()
    top = lax.broadcasted_iota(jnp.int32, (8, 256), 0) < 4
    for p in range(PAIRS):
        for y in range(2):
            halves = []
            for x in (2 * y, 2 * y + 1):
                a = land[0, x, 16 * (p // 2) : 16 * (p // 2) + 16].astype(F32)[8 * (p % 2) : 8 * (p % 2) + 8]
                b = land[1, x, 16 * (p // 2) : 16 * (p // 2) + 16].astype(F32)[8 * (p % 2) : 8 * (p % 2) + 8]
                first = jnp.where(top, a, pltpu.roll(b, 4, 0))
                second = jnp.where(top, pltpu.roll(a, 4, 0), b)
                halves.append(jnp.concatenate([first, second], axis=1))
            base = 32 * p + 16 * y
            out_ref[base : base + 16, :] = jnp.concatenate(halves, axis=0).astype(BF16)

    for n in range(2):
        lists(n).wait_send()
    for i, r in group:
        swap(i, r).wait_send()
        back(i, r).wait_send()
    for j in range(SLICES):
        for way in range(2):
            for step in range(1, HOPS + 1):
                end_hop(j, way, step)


def shards(strain, band_taper, pair_list, pair_counts):
    forward, forward_turn, lag, lag_turn, inverse = (jnp.asarray(t) for t in tables())
    pairs = pair_list.transpose(0, 2, 1).reshape(2, PAIRS)
    operands = (
        strain.reshape(CHAN, SAMP),
        band_taper.reshape(1, NF),
        inverse,
        forward_turn,
        forward,
        lag,
        lag_turn,
        pairs,
        pair_counts,
    )
    dma = pltpu.SemaphoreType.DMA
    window = pltpu.VMEM((2 * HOPS + 1, 2, 16, 512), BF16)
    result = pltpu.VMEM((SLICES, 48, 256), BF16)
    stacks = pl.pallas_call(
        kernel,
        out_shape=jax.ShapeDtypeStruct((PAIRS * CHAN, 512), BF16),
        in_specs=[pl.BlockSpec(memory_space=pltpu.HBM)] * len(operands),
        out_specs=pl.BlockSpec(memory_space=pltpu.VMEM),
        scratch_shapes=[pltpu.VMEM(v.shape, v.dtype) for v in operands[:7]]
        + [
            pltpu.SMEM((2, PAIRS), jnp.int32),
            pltpu.SMEM((1,), jnp.int32),
            pltpu.SMEM((2, PAIRS), jnp.int32),
            pltpu.SMEM((1,), jnp.int32),
            pltpu.VMEM((480, 1024), BF16),
            pltpu.VMEM((2, SLICES, 16, 512), BF16),
            window,
            window,
            window,
            window,
            pltpu.VMEM((2, PAIRS, 8, 512), F32),
            pltpu.VMEM((2, PAIRS, 8, 512), F32),
            pltpu.VMEM((2, 4, 48, 256), BF16),
            result,
            result,
            pltpu.VMEM((2, SLICES, 48, 256), BF16),
            dma((len(operands),)),
            dma((2,)),
            dma((2,)),
            dma((SLICES, 2)),
            dma((SLICES, 2)),
            dma((SLICES, 2, HOPS)),
            dma((SLICES, 2, HOPS)),
            dma((SLICES, 2)),
            dma((SLICES, 2)),
        ],
        compiler_params=pltpu.CompilerParams(
            collective_id=0, has_side_effects=True, vmem_limit_bytes=60 * 1024 * 1024
        ),
    )(*operands)
    return stacks.reshape(PAIRS, CHAN, 512).transpose(2, 0, 1)


def solution(mesh):
    in_specs = (P("cuts", "chan", None), P(), P("chan", None, None), P("chan"))
    out_specs = P("cuts", "chan", None)
    return jax.shard_map(shards, mesh=mesh, in_specs=in_specs, out_specs=out_specs, check_vma=False)
```

```python
import math

import jax
import jax.numpy as jnp
import ml_dtypes
import numpy as np
from jax import lax
from jax.experimental import pallas as pl
from jax.experimental.pallas import tpu as pltpu
from jax.sharding import PartitionSpec as P

SAMP = 8192
F0 = 32
NF = 960
SMOOTH = 32
PAIRS = 6
CHAN = 32
SLICES = 4
HOPS = 4
SLOTS = 2 * (2 * HOPS + 1)
MESH = pl.DeviceIdType.MESH
F32 = jnp.float32
BF16 = jnp.bfloat16
ROOT_HALF = math.sqrt(0.5)


def tables():
    n2 = np.arange(1024)
    k2 = np.arange(128)
    angle = 2 * np.pi * ((n2[:, None] * k2[None, :]) % 1024) / 1024
    forward = np.concatenate([np.cos(angle), np.sin(angle)], axis=1).astype(ml_dtypes.bfloat16)
    k1 = np.arange(8)
    angle = 2 * np.pi * k1[:, None] * n2[None, :] / SAMP
    forward_turn = np.concatenate([np.cos(angle), np.sin(angle)], axis=0).astype(np.float32)
    t1 = np.arange(256)
    angle = 2 * np.pi * ((k2[:, None] * t1[None, :]) % 256) / 256
    c, s = np.cos(angle), np.sin(angle)
    lag = np.block([[c, s], [-s, c]]).astype(ml_dtypes.bfloat16)
    angle = 2 * np.pi * k1[:, None] * t1[None, :] / 2048
    gain = ((-1.0) ** k1)[:, None] / math.sqrt(NF)
    turn = np.stack([np.cos(angle) * gain, np.sin(angle) * gain])
    turn = np.repeat(turn.reshape(2, 2, 4, 1, 256), 4, axis=3)
    lag_turn = turn.transpose(0, 2, 1, 3, 4).reshape(2, 4, 8, 256).astype(np.float32)
    bins = np.arange(NF)
    count = np.minimum(bins + SMOOTH, NF - 1) - np.maximum(bins - SMOOTH, 0) + 1
    inverse = np.ones(1024)
    inverse[F0 : F0 + NF] = 1.0 / count
    inverse = inverse.reshape(128, 8).T.astype(np.float32)
    narrow = np.concatenate([forward, lag[:, :256], lag[:, 256:]], axis=0)
    wide = np.zeros((160, 1024), np.float32)
    wide[:16] = forward_turn
    wide[16:32] = lag_turn.transpose(0, 2, 1, 3).reshape(16, 1024)
    wide[32:40, :128] = inverse
    return narrow, wide


def kernel(
    x_hbm,
    taper_hbm,
    narrow_hbm,
    wide_hbm,
    pairs_hbm,
    count_hbm,
    out_ref,
    x_ref,
    taper_ref,
    wide_ref,
    ftab_ref,
    ltab_ref,
    my_pairs,
    my_count,
    its_pairs,
    its_count,
    y_ref,
    stage,
    win0,
    win1,
    win2,
    win3,
    cross_re,
    cross_im,
    lhs_ref,
    sbuf0,
    sbuf1,
    land,
    load_sem,
    list_send,
    list_recv,
    swap_send,
    swap_recv,
    near_send,
    near_recv,
    hop_send,
    hop_recv,
    back_send,
    back_recv,
):
    win, sbuf = (win0, win1, win2, win3), (sbuf0, sbuf1)
    blocks = lax.axis_size("chan")
    me = lax.axis_index("chan")
    cut = lax.axis_index("cuts")
    core = lax.rem(me, 2)
    chip = me // 2
    chips = blocks // 2
    other = me + 1 - 2 * core

    def at(chan, cuts):
        return {"chan": chan, "cuts": cuts}

    def peer(i):
        return lax.rem(cut + i, SLICES)

    group = [(i, r) for i in range(SLICES) for r in range(2) if (i, r) != (0, 0)]

    def member(i, r):
        return at(other if r else me, peer(i))

    def beside(i, r, way):
        return at((other if r else me) + (2, -2)[way], peer(i))

    barrier = pltpu.get_barrier_semaphore()
    for i, r in group:
        pl.semaphore_signal(barrier, inc=1, device_id=member(i, r), device_id_type=MESH)

    whole = [(i, r) for i in (0, 1, 3, 2) for r in range(2)]
    reaches = (chip + 1 < chips, chip >= 1)
    for way in range(2):

        @pl.when(reaches[way])
        def _(way=way):
            for i, r in whole:
                pl.semaphore_signal(barrier, inc=1, device_id=beside(i, r, way), device_id_type=MESH)

    loads = []
    for n, (src, dst) in enumerate(
        [
            (x_hbm, x_ref),
            (wide_hbm.at[0:40], wide_ref),
            (narrow_hbm.at[0:1024], ftab_ref),
            (taper_hbm, taper_ref),
            (narrow_hbm.at[1024:1280], ltab_ref.at[0]),
            (narrow_hbm.at[1280:1536], ltab_ref.at[1]),
            (pairs_hbm, my_pairs),
            (count_hbm, my_count),
        ]
    ):
        loads.append(pltpu.make_async_copy(src, dst, load_sem.at[n]))
        loads[-1].start()

    def taper_rows():
        row = lax.broadcasted_iota(jnp.int32, (8, NF), 0)
        bins = lax.broadcasted_iota(jnp.int32, (8, NF), 1)
        rest = jnp.where(lax.rem(bins, 8) == row, jnp.broadcast_to(taper_ref[...], (8, NF)), 0.0)
        terms = []
        for _ in range(3):
            term = rest.astype(BF16)
            rest = rest - term.astype(F32)
            terms.append(term.astype(F32))
        terms.append(jnp.zeros_like(rest))
        bins = lax.broadcasted_iota(jnp.int32, (NF, 128), 0)
        lanes = lax.broadcasted_iota(jnp.int32, (NF, 128), 1)
        pick = jnp.where(bins // 8 == lanes - F0 // 8, 1.0, 0.0).astype(BF16)
        g = jnp.dot(jnp.concatenate(terms, axis=0).astype(BF16), pick, preferred_element_type=F32)
        return g[0:8] + g[8:16] + g[16:24]

    loads[3].wait()
    taper = taper_rows()

    def butterflies(j, carry):
        o = pl.multiple_of(j * 128, 128)
        x = [x_ref[:, pl.ds(pl.multiple_of(n1 * 1024 + o, 128), 128)].astype(F32) for n1 in range(8)]
        s = [x[n] + x[n + 4] for n in range(4)]
        d = [x[n] - x[n + 4] for n in range(4)]
        e0, e1 = s[0] + s[2], s[1] + s[3]
        dm, dp = (d[1] - d[3]) * ROOT_HALF, (d[1] + d[3]) * ROOT_HALF
        z1 = (d[0] + dm, -(d[2] + dp))
        z3 = (d[0] - dm, d[2] - dp)
        z2 = (s[0] - s[2], s[3] - s[1])
        y_ref[0:32, pl.ds(o, 128)] = (e0 + e1).astype(BF16)
        z = {1: z1, 2: z2, 3: z3, 4: (e0 - e1, None), 5: (z3[0], -z3[1]), 6: (z2[0], -z2[1]), 7: (z1[0], -z1[1])}
        for k1 in range(1, 8):
            c = wide_ref[k1 : k1 + 1, pl.ds(o, 128)]
            q = wide_ref[8 + k1 : 9 + k1, pl.ds(o, 128)]
            re, im = z[k1]
            if im is None:
                yr, yi = re * c, -(re * q)
            else:
                yr, yi = re * c + im * q, im * c - re * q
            base = 32 + 64 * (k1 - 1)
            y_ref[base : base + 32, pl.ds(o, 128)] = yr.astype(BF16)
            y_ref[base + 32 : base + 64, pl.ds(o, 128)] = yi.astype(BF16)
        return carry

    loads[0].wait()
    loads[1].wait()
    lax.fori_loop(0, 8, butterflies, 0)
    loads[2].wait()
    r = jnp.dot(y_ref[...], ftab_ref[...], preferred_element_type=F32)
    re = [r[0:32, :128]]
    im = [-r[0:32, 128:]]
    for k1 in range(1, 8):
        base = 32 + 64 * (k1 - 1)
        a, b = r[base : base + 32], r[base + 32 : base + 64]
        re.append(a[:, :128] + b[:, 128:])
        im.append(b[:, :128] - a[:, 128:])

    lane = lax.broadcasted_iota(jnp.int32, (CHAN, 128), 1)
    valid = (lane >= F0 // 8) & (lane < (F0 + NF) // 8)
    mag = [jnp.where(valid, jnp.sqrt(re[k] * re[k] + im[k] * im[k]), 0.0) for k in range(8)]
    low = [mag[0]]
    for k in range(1, 8):
        low.append(low[-1] + mag[k])
    high = [mag[7]]
    for k in range(6, -1, -1):
        high.append(high[-1] + mag[k])
    high = high[::-1]
    total = low[7]
    middle = total
    for step in range(1, 4):
        middle = middle + pltpu.roll(total, step, 1) + pltpu.roll(total, 128 - step, 1)
    upper = lax.broadcasted_iota(jnp.int32, (4, 8, 128), 1) < 4
    for k in range(8):
        level = (middle + pltpu.roll(high[k], 4, 1) + pltpu.roll(low[k], 124, 1)) * wide_ref[32 + k : 33 + k, 0:128]
        factor = taper[k : k + 1, :] / (level + 1e-6)
        re[k] = (re[k] * factor).reshape(4, 8, 128)
        im[k] = (im[k] * factor).reshape(4, 8, 128)
    for k in range(4):
        for h in range(2):
            rows = []
            for part in (re, im):
                a, b = part[k], part[k + 4]
                if h == 0:
                    rows.append(jnp.where(upper, a, pltpu.roll(b, 4, 1)))
                else:
                    rows.append(jnp.where(upper, pltpu.roll(a, 4, 1), b))
            stage[h, :, :, k * 128 : (k + 1) * 128] = jnp.concatenate(rows, axis=1).astype(BF16)

    pl.semaphore_wait(barrier, 7 + jnp.where(reaches[0], 8, 0) + jnp.where(reaches[1], 8, 0))

    def swap(i, r):
        return pltpu.make_async_remote_copy(
            src_ref=stage.at[1 - core if r else core, peer(i)],
            dst_ref=win[(SLICES - i) % SLICES].at[HOPS, core],
            send_sem=swap_send.at[i, r],
            recv_sem=swap_recv.at[i, r],
            device_id=member(i, r),
            device_id_type=MESH,
        )

    def near(i, r, way):
        return pltpu.make_async_remote_copy(
            src_ref=stage.at[1 - core if r else core, peer(i)],
            dst_ref=win[(SLICES - i) % SLICES].at[HOPS + (-1, 1)[way], core],
            send_sem=near_send.at[i, r, way],
            recv_sem=near_recv.at[i, r, way],
            device_id=beside(i, r, way),
            device_id_type=MESH,
        )

    def hop(j, way, step):
        sign = -1 if way == 0 else 1
        return pltpu.make_async_remote_copy(
            src_ref=win[j].at[HOPS + sign * (step - 1)],
            dst_ref=win[j].at[HOPS + sign * step],
            send_sem=hop_send.at[j, way, step - 2],
            recv_sem=hop_recv.at[j, way, step - 2],
            device_id=at(me - 2 * sign, cut),
            device_id_type=MESH,
        )

    def send_hop(j, way, step):
        here = chip >= step - 1 if way == 0 else chip + step - 1 < chips

        @pl.when(here & reaches[way])
        def _():
            hop(j, way, step).start()

    def end_hop(j, way, step):
        here = chip >= step - 1 if way == 0 else chip + step - 1 < chips

        @pl.when(here & reaches[way])
        def _():
            hop(j, way, step).wait_send()

    def take_hop(j, way, step):
        @pl.when(chip >= step if way == 0 else chip + step < chips)
        def _():
            if step == 1:
                for r in range(2):
                    near((SLICES - j) % SLICES, r, way).wait_recv()
            else:
                hop(j, way, step).wait_recv()

    def back(i, r):
        return pltpu.make_async_remote_copy(
            src_ref=sbuf[r].at[peer(i)],
            dst_ref=land.at[core, cut],
            send_sem=back_send.at[i, r],
            recv_sem=back_recv.at[i, r],
            device_id=member(i, r),
            device_id_type=MESH,
        )

    def lists(n):
        src, dst = ((pairs_hbm, its_pairs), (count_hbm, its_count))[n]
        return pltpu.make_async_remote_copy(
            src_ref=src,
            dst_ref=dst,
            send_sem=list_send.at[n],
            recv_sem=list_recv.at[n],
            device_id=at(other, cut),
            device_id_type=MESH,
        )

    order = (0, 1, 3, 2)
    for i in (0, 3, 1, 2):
        for way in range(2):

            @pl.when(reaches[way])
            def _(way=way, i=i):
                for r in range(2):
                    near(i, r, way).start()

    for i, r in group:
        swap(i, r).start()
    win[0][HOPS, core] = stage[core, cut]
    for n in range(2):
        lists(n).start()
    for n in (4, 5, 6, 7):
        loads[n].wait()

    def add_slice(j, fresh):
        first = me - core

        def pair(p, carry):
            for r, pairs in ((0, my_pairs), (1, its_pairs)):
                a_slot = jnp.clip(pairs[0, p] - first + 2 * HOPS, 0, SLOTS - 1)
                b_slot = jnp.clip(pairs[1, p] - first + 2 * HOPS, 0, SLOTS - 1)
                a = win[j][a_slot // 2, lax.rem(a_slot, 2)].astype(F32)
                b = win[j][b_slot // 2, lax.rem(b_slot, 2)].astype(F32)
                ar, ai, br, bi = a[:8], a[8:], b[:8], b[8:]
                tr, ti = ar * br + ai * bi, ai * br - ar * bi
                if not fresh:
                    tr, ti = tr + cross_re[r, p], ti + cross_im[r, p]
                cross_re[r, p] = tr
                cross_im[r, p] = ti
            return carry

        lax.fori_loop(0, PAIRS, pair, 0)

    sublane = lax.broadcasted_iota(jnp.int32, (1, 8, 1), 1) < 4

    def correlate(r, count_ref):
        live = [jnp.where(p < count_ref[0], 1.0, 0.0).astype(F32) for p in range(PAIRS)]
        for q in range(PAIRS // 2):
            cr = jnp.concatenate([cross_re[r, 2 * q + e] * live[2 * q + e] for e in range(2)], axis=0).astype(BF16)
            ci = jnp.concatenate([cross_im[r, 2 * q + e] * live[2 * q + e] for e in range(2)], axis=0).astype(BF16)
            for k in range(4):
                lhs_ref[r, k, 16 * q : 16 * q + 16, 0:128] = cr[:, k * 128 : (k + 1) * 128]
                lhs_ref[r, k, 16 * q : 16 * q + 16, 128:256] = ci[:, k * 128 : (k + 1) * 128]
        lhs = lhs_ref[r].reshape(4 * 48, 256)
        vr = jnp.dot(lhs, ltab_ref[0], preferred_element_type=F32)
        vi = jnp.dot(lhs, ltab_ref[1], preferred_element_type=F32)
        parts = []
        for k in range(4):
            dr = vr[48 * k : 48 * (k + 1)].reshape(PAIRS, 8, 256)
            di = vi[48 * k : 48 * (k + 1)].reshape(PAIRS, 8, 256)
            c = wide_ref[16:24, 256 * k : 256 * (k + 1)][None]
            s = wide_ref[24:32, 256 * k : 256 * (k + 1)][None]
            tr, ti = dr * c - di * s, dr * s + di * c
            tr = jnp.where(sublane, tr, -tr) + pltpu.roll(tr, 4, 1)
            ti = jnp.where(sublane, ti, -ti) + pltpu.roll(ti, 4, 1)
            parts.append((tr, ti))
        r0 = parts[0][0]
        c1 = jnp.where(sublane, 1.0, ROOT_HALF)
        c3 = jnp.where(sublane, 1.0, -ROOT_HALF)
        s13 = jnp.where(sublane, 0.0, ROOT_HALF)
        r1, i1 = parts[1][0] * c1 - parts[1][1] * s13, parts[1][0] * s13 + parts[1][1] * c1
        r2 = jnp.where(sublane, parts[2][0], -parts[2][1])
        r3, i3 = parts[3][0] * c3 - parts[3][1] * s13, parts[3][0] * s13 + parts[3][1] * c3
        plus, minus, even, odd = r0 + r2, r0 - r2, r1 + r3, i1 - i3
        for m, value in enumerate((plus + even, minus - odd, plus - even, minus + odd)):
            sbuf[r][m] = value.reshape(48, 256).astype(BF16)

    for step in range(1, HOPS + 1):
        if step == 2:
            for i, r in group:
                swap(i, r).wait_recv()
            for n in range(2):
                lists(n).wait_recv()
        for j in order:
            for way in range(2):
                take_hop(j, way, step)
                if step < HOPS:
                    send_hop(j, way, step + 1)
            if step == HOPS:
                add_slice(j, j == order[0])
    correlate(1, its_count)
    for i in (2, 1, 3, 0):
        back(i, 1).start()
    correlate(0, my_count)
    for i in (2, 1, 3):
        back(i, 0).start()
    land[core, cut] = sbuf[0][cut]

    for i, r in group:
        back(i, r).wait_recv()
    top = lax.broadcasted_iota(jnp.int32, (8, 256), 0) < 4
    for p in range(PAIRS):
        for y in range(2):
            halves = []
            for x in (2 * y, 2 * y + 1):
                a = land[0, x, 16 * (p // 2) : 16 * (p // 2) + 16].astype(F32)[8 * (p % 2) : 8 * (p % 2) + 8]
                b = land[1, x, 16 * (p // 2) : 16 * (p // 2) + 16].astype(F32)[8 * (p % 2) : 8 * (p % 2) + 8]
                first = jnp.where(top, a, pltpu.roll(b, 4, 0))
                second = jnp.where(top, pltpu.roll(a, 4, 0), b)
                halves.append(jnp.concatenate([first, second], axis=1))
            base = 32 * p + 16 * y
            out_ref[base : base + 16, :] = jnp.concatenate(halves, axis=0).astype(BF16)

    for n in range(2):
        lists(n).wait_send()
    for i, r in group:
        swap(i, r).wait_send()
        back(i, r).wait_send()
    for j in range(SLICES):
        for way in range(2):
            for step in range(2, HOPS + 1):
                end_hop(j, way, step)
    for way in range(2):

        @pl.when(reaches[way])
        def _(way=way):
            for i, r in whole:
                near(i, r, way).wait_send()


def shards(strain, band_taper, pair_list, pair_counts):
    narrow, wide = (jnp.asarray(t) for t in tables())
    pairs = pair_list.transpose(0, 2, 1).reshape(2, PAIRS)
    operands = (
        strain.reshape(CHAN, SAMP),
        band_taper.reshape(1, NF),
        narrow,
        wide,
        pairs,
        pair_counts,
    )
    dma = pltpu.SemaphoreType.DMA
    window = pltpu.VMEM((2 * HOPS + 1, 2, 16, 512), BF16)
    result = pltpu.VMEM((SLICES, 48, 256), BF16)
    stacks = pl.pallas_call(
        kernel,
        out_shape=jax.ShapeDtypeStruct((PAIRS * CHAN, 512), BF16),
        in_specs=[pl.BlockSpec(memory_space=pltpu.HBM)] * len(operands),
        out_specs=pl.BlockSpec(memory_space=pltpu.VMEM),
        scratch_shapes=[
            pltpu.VMEM((CHAN, SAMP), BF16),
            pltpu.VMEM((1, NF), F32),
            pltpu.VMEM((40, 1024), F32),
            pltpu.VMEM((1024, 256), BF16),
            pltpu.VMEM((2, 256, 256), BF16),
            pltpu.SMEM((2, PAIRS), jnp.int32),
            pltpu.SMEM((1,), jnp.int32),
            pltpu.SMEM((2, PAIRS), jnp.int32),
            pltpu.SMEM((1,), jnp.int32),
            pltpu.VMEM((480, 1024), BF16),
            pltpu.VMEM((2, SLICES, 16, 512), BF16),
            window,
            window,
            window,
            window,
            pltpu.VMEM((2, PAIRS, 8, 512), F32),
            pltpu.VMEM((2, PAIRS, 8, 512), F32),
            pltpu.VMEM((2, 4, 48, 256), BF16),
            result,
            result,
            pltpu.VMEM((2, SLICES, 48, 256), BF16),
            dma((8,)),
            dma((2,)),
            dma((2,)),
            dma((SLICES, 2)),
            dma((SLICES, 2)),
            dma((SLICES, 2, 2)),
            dma((SLICES, 2, 2)),
            dma((SLICES, 2, HOPS - 1)),
            dma((SLICES, 2, HOPS - 1)),
            dma((SLICES, 2)),
            dma((SLICES, 2)),
        ],
        compiler_params=pltpu.CompilerParams(
            collective_id=0, has_side_effects=True, vmem_limit_bytes=48 * 1024 * 1024
        ),
    )(*(pltpu.with_memory_space_constraint(v, pltpu.HBM) for v in operands[:-1]), pair_counts)
    return stacks.reshape(PAIRS, CHAN, 512).transpose(2, 0, 1)


def solution(mesh):
    in_specs = (P("cuts", "chan", None), P(), P("chan", None, None), P("chan"))
    out_specs = P("cuts", "chan", None)
    return jax.shard_map(shards, mesh=mesh, in_specs=in_specs, out_specs=out_specs, check_vma=False)
```

```python
import math

import jax
import jax.numpy as jnp
import ml_dtypes
import numpy as np
from jax import lax
from jax.experimental import pallas as pl
from jax.experimental.pallas import tpu as pltpu
from jax.sharding import PartitionSpec as P

SAMP = 8192
F0 = 32
NF = 960
SMOOTH = 32
PAIRS = 6
CHAN = 32
SLICES = 4
HOPS = 4
ROW = 8
SLOTS = 2 * (2 * HOPS + 1)
MESH = pl.DeviceIdType.MESH
F32 = jnp.float32
BF16 = jnp.bfloat16
ROOT_HALF = math.sqrt(0.5)


def tables():
    n2 = np.arange(1024)
    k2 = np.arange(128)
    angle = 2 * np.pi * ((n2[:, None] * k2[None, :]) % 1024) / 1024
    forward = np.concatenate([np.cos(angle), np.sin(angle)], axis=1).astype(ml_dtypes.bfloat16)
    k1 = np.arange(8)
    angle = 2 * np.pi * k1[:, None] * n2[None, :] / SAMP
    forward_turn = np.concatenate([np.cos(angle), np.sin(angle)], axis=0).astype(np.float32)
    t1 = np.arange(256)
    angle = 2 * np.pi * ((k2[:, None] * t1[None, :]) % 256) / 256
    c, s = np.cos(angle), np.sin(angle)
    lag = np.block([[c, s], [-s, c]]).astype(ml_dtypes.bfloat16)
    angle = 2 * np.pi * k1[:, None] * t1[None, :] / 2048
    gain = ((-1.0) ** k1)[:, None] / math.sqrt(NF)
    turn = np.stack([np.cos(angle) * gain, np.sin(angle) * gain])
    turn = np.repeat(turn.reshape(2, 2, 4, 1, 256), 4, axis=3)
    lag_turn = turn.transpose(0, 2, 1, 3, 4).reshape(2, 4, 8, 256).astype(np.float32)
    bins = np.arange(NF)
    count = np.minimum(bins + SMOOTH, NF - 1) - np.maximum(bins - SMOOTH, 0) + 1
    inverse = np.ones(1024)
    inverse[F0 : F0 + NF] = 1.0 / count
    inverse = inverse.reshape(128, 8).T.astype(np.float32)
    narrow = np.concatenate([forward, lag[:, :256], lag[:, 256:]], axis=0)
    wide = np.zeros((160, 1024), np.float32)
    wide[:16] = forward_turn
    wide[16:32] = lag_turn.transpose(0, 2, 1, 3).reshape(16, 1024)
    wide[32:40, :128] = inverse
    return narrow, wide


def kernel(
    x_hbm,
    taper_hbm,
    narrow_hbm,
    wide_hbm,
    pairs_hbm,
    count_hbm,
    out_ref,
    x_ref,
    taper_ref,
    wide_ref,
    ftab_ref,
    ltab_ref,
    my_pairs,
    my_count,
    its_pairs,
    its_count,
    y_ref,
    stage,
    win0,
    win1,
    win2,
    win3,
    cross_re,
    cross_im,
    lhs_ref,
    sbuf0,
    sbuf1,
    land,
    load_sem,
    list_send,
    list_recv,
    swap_send,
    swap_recv,
    near_send,
    near_recv,
    hop_send,
    hop_recv,
    back_send,
    back_recv,
):
    win, sbuf = (win0, win1, win2, win3), (sbuf0, sbuf1)
    blocks = lax.axis_size("chan")
    me = lax.axis_index("chan")
    cut = lax.axis_index("cuts")
    core = lax.rem(me, 2)
    chip = me // 2
    chips = blocks // 2
    other = me + 1 - 2 * core

    def at(chan, cuts):
        return {"chan": chan, "cuts": cuts}

    def peer(i):
        return lax.rem(cut + i, SLICES)

    group = [(i, r) for i in range(SLICES) for r in range(2) if (i, r) != (0, 0)]

    def member(i, r):
        return at(other if r else me, peer(i))

    def beside(i, r, way):
        return at((other if r else me) + 2 - 4 * way, peer(i))

    barrier = pltpu.get_barrier_semaphore()
    for i, r in group:
        pl.semaphore_signal(barrier, inc=1, device_id=member(i, r), device_id_type=MESH)

    whole = [(i, r) for i in (0, 1, 3, 2) for r in range(2)]
    reaches = (chip + 1 < chips, chip >= 1)
    for way in range(2):

        @pl.when(reaches[way])
        def _(way=way):
            for i, r in whole:
                pl.semaphore_signal(barrier, inc=1, device_id=beside(i, r, way), device_id_type=MESH)

    loads = []
    for n, (src, dst) in enumerate(
        [
            (x_hbm, x_ref),
            (wide_hbm.at[0:40], wide_ref),
            (narrow_hbm.at[0:1024], ftab_ref),
            (taper_hbm, taper_ref),
            (narrow_hbm.at[1024:1280], ltab_ref.at[0]),
            (narrow_hbm.at[1280:1536], ltab_ref.at[1]),
            (pairs_hbm, my_pairs),
            (count_hbm, my_count),
        ]
    ):
        loads.append(pltpu.make_async_copy(src, dst, load_sem.at[n]))
        loads[-1].start()

    def taper_rows():
        row = lax.broadcasted_iota(jnp.int32, (8, NF), 0)
        bins = lax.broadcasted_iota(jnp.int32, (8, NF), 1)
        rest = jnp.where(lax.rem(bins, 8) == row, jnp.broadcast_to(taper_ref[...], (8, NF)), 0.0)
        terms = []
        for _ in range(3):
            term = rest.astype(BF16)
            rest = rest - term.astype(F32)
            terms.append(term.astype(F32))
        terms.append(jnp.zeros_like(rest))
        bins = lax.broadcasted_iota(jnp.int32, (NF, 128), 0)
        lanes = lax.broadcasted_iota(jnp.int32, (NF, 128), 1)
        pick = jnp.where(bins // 8 == lanes - F0 // 8, 1.0, 0.0).astype(BF16)
        g = jnp.dot(jnp.concatenate(terms, axis=0).astype(BF16), pick, preferred_element_type=F32)
        return g[0:8] + g[8:16] + g[16:24]

    loads[3].wait()
    taper = taper_rows()

    def butterflies(j, carry):
        o = pl.multiple_of(j * 128, 128)
        x = [x_ref[:, pl.ds(pl.multiple_of(n1 * 1024 + o, 128), 128)].astype(F32) for n1 in range(8)]
        s = [x[n] + x[n + 4] for n in range(4)]
        d = [x[n] - x[n + 4] for n in range(4)]
        e0, e1 = s[0] + s[2], s[1] + s[3]
        dm, dp = (d[1] - d[3]) * ROOT_HALF, (d[1] + d[3]) * ROOT_HALF
        z1 = (d[0] + dm, -(d[2] + dp))
        z3 = (d[0] - dm, d[2] - dp)
        z2 = (s[0] - s[2], s[3] - s[1])
        y_ref[0:32, pl.ds(o, 128)] = (e0 + e1).astype(BF16)
        z = {1: z1, 2: z2, 3: z3, 4: (e0 - e1, None), 5: (z3[0], -z3[1]), 6: (z2[0], -z2[1]), 7: (z1[0], -z1[1])}
        for k1 in range(1, 8):
            c = wide_ref[k1 : k1 + 1, pl.ds(o, 128)]
            q = wide_ref[8 + k1 : 9 + k1, pl.ds(o, 128)]
            re, im = z[k1]
            if im is None:
                yr, yi = re * c, -(re * q)
            else:
                yr, yi = re * c + im * q, im * c - re * q
            base = 32 + 64 * (k1 - 1)
            y_ref[base : base + 32, pl.ds(o, 128)] = yr.astype(BF16)
            y_ref[base + 32 : base + 64, pl.ds(o, 128)] = yi.astype(BF16)
        return carry

    loads[0].wait()
    loads[1].wait()
    lax.fori_loop(0, 8, butterflies, 0)
    loads[2].wait()
    r = jnp.dot(y_ref[...], ftab_ref[...], preferred_element_type=F32)
    re = [r[0:32, :128]]
    im = [-r[0:32, 128:]]
    for k1 in range(1, 8):
        base = 32 + 64 * (k1 - 1)
        a, b = r[base : base + 32], r[base + 32 : base + 64]
        re.append(a[:, :128] + b[:, 128:])
        im.append(b[:, :128] - a[:, 128:])

    lane = lax.broadcasted_iota(jnp.int32, (CHAN, 128), 1)
    valid = (lane >= F0 // 8) & (lane < (F0 + NF) // 8)
    mag = [jnp.where(valid, jnp.sqrt(re[k] * re[k] + im[k] * im[k]), 0.0) for k in range(8)]
    low = [mag[0]]
    for k in range(1, 8):
        low.append(low[-1] + mag[k])
    high = [mag[7]]
    for k in range(6, -1, -1):
        high.append(high[-1] + mag[k])
    high = high[::-1]
    total = low[7]
    middle = total
    for step in range(1, 4):
        middle = middle + pltpu.roll(total, step, 1) + pltpu.roll(total, 128 - step, 1)
    upper = lax.broadcasted_iota(jnp.int32, (4, 8, 128), 1) < 4
    for k in range(8):
        level = (middle + pltpu.roll(high[k], 4, 1) + pltpu.roll(low[k], 124, 1)) * wide_ref[32 + k : 33 + k, 0:128]
        factor = taper[k : k + 1, :] / (level + 1e-6)
        re[k] = (re[k] * factor).reshape(4, 8, 128)
        im[k] = (im[k] * factor).reshape(4, 8, 128)
    for k in range(4):
        for h in range(2):
            rows = []
            for part in (re, im):
                a, b = part[k], part[k + 4]
                if h == 0:
                    rows.append(jnp.where(upper, a, pltpu.roll(b, 4, 1)))
                else:
                    rows.append(jnp.where(upper, pltpu.roll(a, 4, 1), b))
            stage[h, :, :, k * 128 : (k + 1) * 128] = jnp.concatenate(rows, axis=1).astype(BF16)

    pl.semaphore_wait(barrier, 7 + jnp.where(reaches[0], 8, 0) + jnp.where(reaches[1], 8, 0))

    def swap(i, r):
        return pltpu.make_async_remote_copy(
            src_ref=stage.at[1 - core if r else core, peer(i)],
            dst_ref=win[(SLICES - i) % SLICES].at[HOPS, core],
            send_sem=swap_send.at[i, r],
            recv_sem=swap_recv.at[i, r],
            device_id=member(i, r),
            device_id_type=MESH,
        )

    def near(i, r, way):
        return pltpu.make_async_remote_copy(
            src_ref=stage.at[1 - core if r else core, peer(i)],
            dst_ref=win[(SLICES - i) % SLICES].at[HOPS + 2 * way - 1, core],
            send_sem=near_send.at[i, r, way],
            recv_sem=near_recv.at[i, r, way],
            device_id=beside(i, r, way),
            device_id_type=MESH,
        )

    def hop(j, way, step):
        sign = 2 * way - 1
        return pltpu.make_async_remote_copy(
            src_ref=win[j].at[HOPS + sign * (step - 1)],
            dst_ref=win[j].at[HOPS + sign * step],
            send_sem=hop_send.at[j, way, step - 2],
            recv_sem=hop_recv.at[j, way, step - 2],
            device_id=at(me - 2 * sign, cut),
            device_id_type=MESH,
        )

    def comes(way, step):
        return jnp.where(way == 0, chip, chips - 1 - chip) >= step

    def goes(way, step):
        return comes(way, step - 1) & (jnp.where(way == 0, chips - 1 - chip, chip) >= 1)

    def end_hop(j, way, step):
        @pl.when(goes(way, step))
        def _():
            hop(j, way, step).wait_send()

    def take(j, way, step):
        @pl.when(comes(way, step))
        def _():
            if step == 1:
                for r in range(2):
                    near((SLICES - j) % SLICES, r, way).wait_recv()
            else:
                hop(j, way, step).wait_recv()

        if step < HOPS:

            @pl.when(goes(way, step + 1))
            def _():
                hop(j, way, step + 1).start()

    def back(i, r):
        return pltpu.make_async_remote_copy(
            src_ref=sbuf[r].at[peer(i)],
            dst_ref=land.at[core, cut],
            send_sem=back_send.at[i, r],
            recv_sem=back_recv.at[i, r],
            device_id=member(i, r),
            device_id_type=MESH,
        )

    def lists(n):
        src, dst = ((pairs_hbm, its_pairs), (count_hbm, its_count))[n]
        return pltpu.make_async_remote_copy(
            src_ref=src,
            dst_ref=dst,
            send_sem=list_send.at[n],
            recv_sem=list_recv.at[n],
            device_id=at(other, cut),
            device_id_type=MESH,
        )

    order = (0, 1, 3, 2)
    for i in (0, 3, 1, 2):
        for way in range(2):

            @pl.when(reaches[way])
            def _(way=way, i=i):
                for r in range(2):
                    near(i, r, way).start()

    for i, r in group:
        swap(i, r).start()
    win[0][HOPS, core] = stage[core, cut]
    for n in range(2):
        lists(n).start()
    for n in (4, 5, 6, 7):
        loads[n].wait()

    def add_slice(j, fresh):
        first = me - core

        def pair(p, carry):
            for r, pairs in ((0, my_pairs), (1, its_pairs)):
                a_slot = jnp.clip(pairs[0, p] - first + 2 * HOPS, 0, SLOTS - 1)
                b_slot = jnp.clip(pairs[1, p] - first + 2 * HOPS, 0, SLOTS - 1)
                a = win[j][a_slot // 2, lax.rem(a_slot, 2)].astype(F32)
                b = win[j][b_slot // 2, lax.rem(b_slot, 2)].astype(F32)
                ar, ai, br, bi = a[:8], a[8:], b[:8], b[8:]
                tr, ti = ar * br + ai * bi, ai * br - ar * bi
                if not fresh:
                    tr, ti = tr + cross_re[r, p], ti + cross_im[r, p]
                cross_re[r, p] = tr
                cross_im[r, p] = ti
            return carry

        lax.fori_loop(0, PAIRS, pair, 0)

    sublane = lax.broadcasted_iota(jnp.int32, (1, 8, 1), 1) < 4

    def correlate(r, count_ref):
        live = [jnp.where(p < count_ref[0], 1.0, 0.0).astype(F32) for p in range(PAIRS)]
        for q in range(PAIRS // 2):
            cr = jnp.concatenate([cross_re[r, 2 * q + e] * live[2 * q + e] for e in range(2)], axis=0).astype(BF16)
            ci = jnp.concatenate([cross_im[r, 2 * q + e] * live[2 * q + e] for e in range(2)], axis=0).astype(BF16)
            for k in range(4):
                lhs_ref[r, k, 16 * q : 16 * q + 16, 0:128] = cr[:, k * 128 : (k + 1) * 128]
                lhs_ref[r, k, 16 * q : 16 * q + 16, 128:256] = ci[:, k * 128 : (k + 1) * 128]
        lhs = lhs_ref[r].reshape(4 * 48, 256)
        vr = jnp.dot(lhs, ltab_ref[0], preferred_element_type=F32)
        vi = jnp.dot(lhs, ltab_ref[1], preferred_element_type=F32)
        parts = []
        for k in range(4):
            dr = vr[48 * k : 48 * (k + 1)].reshape(PAIRS, 8, 256)
            di = vi[48 * k : 48 * (k + 1)].reshape(PAIRS, 8, 256)
            c = wide_ref[16:24, 256 * k : 256 * (k + 1)][None]
            s = wide_ref[24:32, 256 * k : 256 * (k + 1)][None]
            tr, ti = dr * c - di * s, dr * s + di * c
            tr = jnp.where(sublane, tr, -tr) + pltpu.roll(tr, 4, 1)
            ti = jnp.where(sublane, ti, -ti) + pltpu.roll(ti, 4, 1)
            parts.append((tr, ti))
        r0 = parts[0][0]
        c1 = jnp.where(sublane, 1.0, ROOT_HALF)
        c3 = jnp.where(sublane, 1.0, -ROOT_HALF)
        s13 = jnp.where(sublane, 0.0, ROOT_HALF)
        r1, i1 = parts[1][0] * c1 - parts[1][1] * s13, parts[1][0] * s13 + parts[1][1] * c1
        r2 = jnp.where(sublane, parts[2][0], -parts[2][1])
        r3, i3 = parts[3][0] * c3 - parts[3][1] * s13, parts[3][0] * s13 + parts[3][1] * c3
        plus, minus, even, odd = r0 + r2, r0 - r2, r1 + r3, i1 - i3
        for m, value in enumerate((plus + even, minus - odd, plus - even, minus + odd)):
            sbuf[r][m] = value.reshape(48, 256).astype(BF16)

    row = lax.rem(chip, ROW)
    sooner = jnp.where(row < 2, 1, 0)
    later = 1 - sooner
    behind = (row == 0) | (row == ROW - 1)
    turns = [(step, j) for step in range(1, HOPS + 1) for j in order]
    for n in range(len(turns) + 1):
        if n == SLICES:
            for i, r in group:
                swap(i, r).wait_recv()
            for e in range(2):
                lists(e).wait_recv()
        if n < len(turns):
            take(turns[n][1], sooner, turns[n][0])

            @pl.when(jnp.logical_not(behind))
            def _(n=n):
                take(turns[n][1], later, turns[n][0])

        if n > 0:

            @pl.when(behind)
            def _(n=n):
                take(turns[n - 1][1], later, turns[n - 1][0])

            if turns[n - 1][0] == HOPS:
                add_slice(turns[n - 1][1], turns[n - 1][1] == order[0])
    correlate(1, its_count)
    for i in (2, 1, 3, 0):
        back(i, 1).start()
    correlate(0, my_count)
    for i in (2, 1, 3):
        back(i, 0).start()
    land[core, cut] = sbuf[0][cut]

    for i, r in group:
        back(i, r).wait_recv()
    top = lax.broadcasted_iota(jnp.int32, (8, 256), 0) < 4
    for p in range(PAIRS):
        for y in range(2):
            halves = []
            for x in (2 * y, 2 * y + 1):
                a = land[0, x, 16 * (p // 2) : 16 * (p // 2) + 16].astype(F32)[8 * (p % 2) : 8 * (p % 2) + 8]
                b = land[1, x, 16 * (p // 2) : 16 * (p // 2) + 16].astype(F32)[8 * (p % 2) : 8 * (p % 2) + 8]
                first = jnp.where(top, a, pltpu.roll(b, 4, 0))
                second = jnp.where(top, pltpu.roll(a, 4, 0), b)
                halves.append(jnp.concatenate([first, second], axis=1))
            base = 32 * p + 16 * y
            out_ref[base : base + 16, :] = jnp.concatenate(halves, axis=0).astype(BF16)

    for n in range(2):
        lists(n).wait_send()
    for i, r in group:
        swap(i, r).wait_send()
        back(i, r).wait_send()
    for j in range(SLICES):
        for way in range(2):
            for step in range(2, HOPS + 1):
                end_hop(j, way, step)
    for way in range(2):

        @pl.when(reaches[way])
        def _(way=way):
            for i, r in whole:
                near(i, r, way).wait_send()


def shards(strain, band_taper, pair_list, pair_counts):
    narrow, wide = (jnp.asarray(t) for t in tables())
    pairs = pair_list.transpose(0, 2, 1).reshape(2, PAIRS)
    operands = (
        strain.reshape(CHAN, SAMP),
        band_taper.reshape(1, NF),
        narrow,
        wide,
        pairs,
        pair_counts,
    )
    dma = pltpu.SemaphoreType.DMA
    window = pltpu.VMEM((2 * HOPS + 1, 2, 16, 512), BF16)
    result = pltpu.VMEM((SLICES, 48, 256), BF16)
    stacks = pl.pallas_call(
        kernel,
        out_shape=jax.ShapeDtypeStruct((PAIRS * CHAN, 512), BF16),
        in_specs=[pl.BlockSpec(memory_space=pltpu.HBM)] * len(operands),
        out_specs=pl.BlockSpec(memory_space=pltpu.VMEM),
        scratch_shapes=[
            pltpu.VMEM((CHAN, SAMP), BF16),
            pltpu.VMEM((1, NF), F32),
            pltpu.VMEM((40, 1024), F32),
            pltpu.VMEM((1024, 256), BF16),
            pltpu.VMEM((2, 256, 256), BF16),
            pltpu.SMEM((2, PAIRS), jnp.int32),
            pltpu.SMEM((1,), jnp.int32),
            pltpu.SMEM((2, PAIRS), jnp.int32),
            pltpu.SMEM((1,), jnp.int32),
            pltpu.VMEM((480, 1024), BF16),
            pltpu.VMEM((2, SLICES, 16, 512), BF16),
            window,
            window,
            window,
            window,
            pltpu.VMEM((2, PAIRS, 8, 512), F32),
            pltpu.VMEM((2, PAIRS, 8, 512), F32),
            pltpu.VMEM((2, 4, 48, 256), BF16),
            result,
            result,
            pltpu.VMEM((2, SLICES, 48, 256), BF16),
            dma((8,)),
            dma((2,)),
            dma((2,)),
            dma((SLICES, 2)),
            dma((SLICES, 2)),
            dma((SLICES, 2, 2)),
            dma((SLICES, 2, 2)),
            dma((SLICES, 2, HOPS - 1)),
            dma((SLICES, 2, HOPS - 1)),
            dma((SLICES, 2)),
            dma((SLICES, 2)),
        ],
        compiler_params=pltpu.CompilerParams(
            collective_id=0, has_side_effects=True, vmem_limit_bytes=48 * 1024 * 1024
        ),
    )(*(pltpu.with_memory_space_constraint(v, pltpu.HBM) for v in operands[:-1]), pair_counts)
    return stacks.reshape(PAIRS, CHAN, 512).transpose(2, 0, 1)


def solution(mesh):
    in_specs = (P("cuts", "chan", None), P(), P("chan", None, None), P("chan"))
    out_specs = P("cuts", "chan", None)
    return jax.shard_map(shards, mesh=mesh, in_specs=in_specs, out_specs=out_specs, check_vma=False)
```

```python
import math

import jax
import jax.numpy as jnp
import ml_dtypes
import numpy as np
from jax import lax
from jax.experimental import pallas as pl
from jax.experimental.pallas import tpu as pltpu
from jax.sharding import PartitionSpec as P

SAMP = 8192
F0 = 32
NF = 960
SMOOTH = 32
PAIRS = 6
CHAN = 32
SLICES = 4
HOPS = 4
ROW = 8
SLOTS = 2 * (2 * HOPS + 1)
MESH = pl.DeviceIdType.MESH
F32 = jnp.float32
BF16 = jnp.bfloat16
ROOT_HALF = math.sqrt(0.5)


def tables():
    n2 = np.arange(1024)
    k2 = np.arange(128)
    angle = 2 * np.pi * ((n2[:, None] * k2[None, :]) % 1024) / 1024
    forward = np.concatenate([np.cos(angle), np.sin(angle)], axis=1).astype(ml_dtypes.bfloat16)
    k1 = np.arange(8)
    angle = 2 * np.pi * k1[:, None] * n2[None, :] / SAMP
    forward_turn = np.concatenate([np.cos(angle), np.sin(angle)], axis=0).astype(np.float32)
    t1 = np.arange(256)
    angle = 2 * np.pi * ((k2[:, None] * t1[None, :]) % 256) / 256
    c, s = np.cos(angle), np.sin(angle)
    lag = np.block([[c, s], [-s, c]]).astype(ml_dtypes.bfloat16)
    angle = 2 * np.pi * k1[:, None] * t1[None, :] / 2048
    gain = ((-1.0) ** k1)[:, None] / math.sqrt(NF)
    turn = np.stack([np.cos(angle) * gain, np.sin(angle) * gain])
    turn = np.repeat(turn.reshape(2, 2, 4, 1, 256), 4, axis=3)
    lag_turn = turn.transpose(0, 2, 1, 3, 4).reshape(2, 4, 8, 256).astype(np.float32)
    bins = np.arange(NF)
    count = np.minimum(bins + SMOOTH, NF - 1) - np.maximum(bins - SMOOTH, 0) + 1
    inverse = np.ones(1024)
    inverse[F0 : F0 + NF] = 1.0 / count
    inverse = inverse.reshape(128, 8).T.astype(np.float32)
    narrow = np.concatenate([forward, lag[:, :256], lag[:, 256:]], axis=0)
    wide = np.zeros((160, 1024), np.float32)
    wide[:16] = forward_turn
    wide[16:32] = lag_turn.transpose(0, 2, 1, 3).reshape(16, 1024)
    wide[32:40, :128] = inverse
    return narrow, wide


def kernel(
    x_hbm,
    taper_hbm,
    narrow_hbm,
    wide_hbm,
    pairs_hbm,
    count_hbm,
    out_ref,
    x_ref,
    taper_ref,
    wide_ref,
    ftab_ref,
    ltab_ref,
    my_pairs,
    my_count,
    its_pairs,
    its_count,
    y_ref,
    r_ref,
    stage,
    win0,
    win1,
    win2,
    win3,
    cross_re,
    cross_im,
    lhs_ref,
    sbuf0,
    sbuf1,
    land,
    load_sem,
    list_send,
    list_recv,
    swap_send,
    swap_recv,
    near_send,
    near_recv,
    hop_send,
    hop_recv,
    back_send,
    back_recv,
):
    win, sbuf = (win0, win1, win2, win3), (sbuf0, sbuf1)
    blocks = lax.axis_size("chan")
    me = lax.axis_index("chan")
    cut = lax.axis_index("cuts")
    core = lax.rem(me, 2)
    chip = me // 2
    chips = blocks // 2
    other = me + 1 - 2 * core

    def at(chan, cuts):
        return {"chan": chan, "cuts": cuts}

    def peer(i):
        return lax.rem(cut + i, SLICES)

    group = [(i, r) for i in range(SLICES) for r in range(2) if (i, r) != (0, 0)]

    def member(i, r):
        return at(other if r else me, peer(i))

    def beside(i, r, way):
        return at((other if r else me) + 2 - 4 * way, peer(i))

    barrier = pltpu.get_barrier_semaphore()
    reaches = (chip + 1 < chips, chip >= 1)
    whole = [(i, r) for i in (2, 1, 3, 0) for r in range(2)]
    for i, r in whole:
        for way in range(2):

            @pl.when(reaches[way])
            def _(i=i, r=r, way=way):
                pl.semaphore_signal(barrier, inc=1, device_id=beside(i, r, way), device_id_type=MESH)

        if (i, r) in group:
            pl.semaphore_signal(barrier, inc=1, device_id=member(i, r), device_id_type=MESH)

    loads = []
    for n, (src, dst) in enumerate(
        [
            (taper_hbm, taper_ref),
            (x_hbm.at[0:16], x_ref.at[0:16]),
            (wide_hbm.at[0:40], wide_ref),
            (x_hbm.at[16:32], x_ref.at[16:32]),
            (narrow_hbm.at[0:1024], ftab_ref),
            (pairs_hbm, my_pairs),
            (count_hbm, my_count),
            (narrow_hbm.at[1024:1280], ltab_ref.at[0]),
            (narrow_hbm.at[1280:1536], ltab_ref.at[1]),
        ]
    ):
        loads.append(pltpu.make_async_copy(src, dst, load_sem.at[n]))
    for n in range(7):
        loads[n].start()

    def taper_rows():
        row = lax.broadcasted_iota(jnp.int32, (8, NF), 0)
        bins = lax.broadcasted_iota(jnp.int32, (8, NF), 1)
        rest = jnp.where(lax.rem(bins, 8) == row, jnp.broadcast_to(taper_ref[...], (8, NF)), 0.0)
        terms = []
        for _ in range(3):
            term = rest.astype(BF16)
            rest = rest - term.astype(F32)
            terms.append(term.astype(F32))
        terms.append(jnp.zeros_like(rest))
        bins = lax.broadcasted_iota(jnp.int32, (NF, 128), 0)
        lanes = lax.broadcasted_iota(jnp.int32, (NF, 128), 1)
        pick = jnp.where(bins // 8 == lanes - F0 // 8, 1.0, 0.0).astype(BF16)
        g = jnp.dot(jnp.concatenate(terms, axis=0).astype(BF16), pick, preferred_element_type=F32)
        return g[0:8] + g[8:16] + g[16:24]

    loads[0].wait()
    taper = taper_rows()

    def butterflies(first, j):
        o = pl.multiple_of(j * 128, 128)
        rows = slice(first, first + 16)
        x = [x_ref[rows, pl.ds(pl.multiple_of(n1 * 1024 + o, 128), 128)].astype(F32) for n1 in range(8)]
        s = [x[n] + x[n + 4] for n in range(4)]
        d = [x[n] - x[n + 4] for n in range(4)]
        e0, e1 = s[0] + s[2], s[1] + s[3]
        dm, dp = (d[1] - d[3]) * ROOT_HALF, (d[1] + d[3]) * ROOT_HALF
        z1 = (d[0] + dm, -(d[2] + dp))
        z3 = (d[0] - dm, d[2] - dp)
        z2 = (s[0] - s[2], s[3] - s[1])
        y_ref[first : first + 16, pl.ds(o, 128)] = (e0 + e1).astype(BF16)
        z = {1: z1, 2: z2, 3: z3, 4: (e0 - e1, None), 5: (z3[0], -z3[1]), 6: (z2[0], -z2[1]), 7: (z1[0], -z1[1])}
        for k1 in range(1, 8):
            c = wide_ref[k1 : k1 + 1, pl.ds(o, 128)]
            q = wide_ref[8 + k1 : 9 + k1, pl.ds(o, 128)]
            re, im = z[k1]
            if im is None:
                yr, yi = re * c, -(re * q)
            else:
                yr, yi = re * c + im * q, im * c - re * q
            base = 32 + 64 * (k1 - 1) + first
            y_ref[base : base + 16, pl.ds(o, 128)] = yr.astype(BF16)
            y_ref[base + 32 : base + 48, pl.ds(o, 128)] = yi.astype(BF16)

    for h in range(2):
        loads[1 + 2 * h].wait()
        if h == 0:
            loads[2].wait()

        def half(j, carry, h=h):
            butterflies(16 * h, j)
            return carry

        lax.fori_loop(0, 8, half, 0)
    loads[4].wait()
    loads[7].start()
    loads[8].start()
    r_ref[...] = jnp.dot(y_ref[...], ftab_ref[...], preferred_element_type=F32)

    lane = lax.broadcasted_iota(jnp.int32, (8, 128), 1)
    valid = (lane >= F0 // 8) & (lane < (F0 + NF) // 8)
    upper = lax.broadcasted_iota(jnp.int32, (8, 128), 0) < 4

    def whiten(i):
        first = pl.multiple_of(8 * peer(i), 8)
        low = r_ref[pl.ds(first, 8), :]
        re, im = [low[:, :128]], [-low[:, 128:]]
        for k1 in range(1, 8):
            a = r_ref[pl.ds(first + 64 * k1 - 32, 8), :]
            b = r_ref[pl.ds(first + 64 * k1, 8), :]
            re.append(a[:, :128] + b[:, 128:])
            im.append(b[:, :128] - a[:, 128:])
        mag = [jnp.where(valid, jnp.sqrt(re[k] * re[k] + im[k] * im[k]), 0.0) for k in range(8)]
        low = [mag[0]]
        for k in range(1, 8):
            low.append(low[-1] + mag[k])
        high = [mag[7]]
        for k in range(6, -1, -1):
            high.append(high[-1] + mag[k])
        high = high[::-1]
        total = low[7]
        middle = total
        for step in range(1, 4):
            middle = middle + pltpu.roll(total, step, 1) + pltpu.roll(total, 128 - step, 1)
        for k in range(8):
            level = (middle + pltpu.roll(high[k], 4, 1) + pltpu.roll(low[k], 124, 1)) * wide_ref[32 + k : 33 + k, 0:128]
            factor = taper[k : k + 1, :] / (level + 1e-6)
            re[k] = re[k] * factor
            im[k] = im[k] * factor
        for k in range(4):
            for h in range(2):
                rows = []
                for part in (re, im):
                    a, b = part[k], part[k + 4]
                    if h == 0:
                        rows.append(jnp.where(upper, a, pltpu.roll(b, 4, 0)))
                    else:
                        rows.append(jnp.where(upper, pltpu.roll(a, 4, 0), b))
                stage[h, i, :, k * 128 : (k + 1) * 128] = jnp.concatenate(rows, axis=0).astype(BF16)

    def swap(i, r):
        return pltpu.make_async_remote_copy(
            src_ref=stage.at[1 - core if r else core, i],
            dst_ref=win[(SLICES - i) % SLICES].at[HOPS, core],
            send_sem=swap_send.at[i, r],
            recv_sem=swap_recv.at[i, r],
            device_id=member(i, r),
            device_id_type=MESH,
        )

    def near(i, r, way):
        return pltpu.make_async_remote_copy(
            src_ref=stage.at[1 - core if r else core, i],
            dst_ref=win[(SLICES - i) % SLICES].at[HOPS + 2 * way - 1, core],
            send_sem=near_send.at[i, r, way],
            recv_sem=near_recv.at[i, r, way],
            device_id=beside(i, r, way),
            device_id_type=MESH,
        )

    def hop(j, way, step):
        sign = 2 * way - 1
        return pltpu.make_async_remote_copy(
            src_ref=win[j].at[HOPS + sign * (step - 1)],
            dst_ref=win[j].at[HOPS + sign * step],
            send_sem=hop_send.at[j, way, step - 2],
            recv_sem=hop_recv.at[j, way, step - 2],
            device_id=at(me - 2 * sign, cut),
            device_id_type=MESH,
        )

    def comes(way, step):
        return jnp.where(way == 0, chip, chips - 1 - chip) >= step

    def goes(way, step):
        return comes(way, step - 1) & (jnp.where(way == 0, chips - 1 - chip, chip) >= 1)

    def end_hop(j, way, step):
        @pl.when(goes(way, step))
        def _():
            hop(j, way, step).wait_send()

    def take(j, way, step):
        @pl.when(comes(way, step))
        def _():
            if step == 1:
                for r in range(2):
                    near((SLICES - j) % SLICES, r, way).wait_recv()
            else:
                hop(j, way, step).wait_recv()

        if step < HOPS:

            @pl.when(goes(way, step + 1))
            def _():
                hop(j, way, step + 1).start()

    def back(i, r):
        return pltpu.make_async_remote_copy(
            src_ref=sbuf[r].at[peer(i)],
            dst_ref=land.at[core, cut],
            send_sem=back_send.at[i, r],
            recv_sem=back_recv.at[i, r],
            device_id=member(i, r),
            device_id_type=MESH,
        )

    def lists(n):
        src, dst = ((pairs_hbm, its_pairs), (count_hbm, its_count))[n]
        return pltpu.make_async_remote_copy(
            src_ref=src,
            dst_ref=dst,
            send_sem=list_send.at[n],
            recv_sem=list_recv.at[n],
            device_id=at(other, cut),
            device_id_type=MESH,
        )

    order = (0, 1, 3, 2)
    for n, i in enumerate((0, 3, 1, 2)):
        whiten(i)
        if n == 0:
            pl.semaphore_wait(barrier, 7 + jnp.where(reaches[0], 8, 0) + jnp.where(reaches[1], 8, 0))
        for way in range(2):

            @pl.when(reaches[way])
            def _(way=way, i=i):
                for r in range(2):
                    near(i, r, way).start()

    win[0][HOPS, core] = stage[core, 0]
    for n in range(2):
        lists(n).start()
    for n in (5, 6, 7, 8):
        loads[n].wait()

    def add_slice(j, fresh):
        first = me - core

        def pair(p, carry):
            for r, pairs in ((0, my_pairs), (1, its_pairs)):
                a_slot = jnp.clip(pairs[0, p] - first + 2 * HOPS, 0, SLOTS - 1)
                b_slot = jnp.clip(pairs[1, p] - first + 2 * HOPS, 0, SLOTS - 1)
                a = win[j][a_slot // 2, lax.rem(a_slot, 2)].astype(F32)
                b = win[j][b_slot // 2, lax.rem(b_slot, 2)].astype(F32)
                ar, ai, br, bi = a[:8], a[8:], b[:8], b[8:]
                tr, ti = ar * br + ai * bi, ai * br - ar * bi
                if not fresh:
                    tr, ti = tr + cross_re[r, p], ti + cross_im[r, p]
                cross_re[r, p] = tr
                cross_im[r, p] = ti
            return carry

        lax.fori_loop(0, PAIRS, pair, 0)

    sublane = lax.broadcasted_iota(jnp.int32, (1, 8, 1), 1) < 4

    def correlate(r, count_ref):
        live = [jnp.where(p < count_ref[0], 1.0, 0.0).astype(F32) for p in range(PAIRS)]
        for q in range(PAIRS // 2):
            cr = jnp.concatenate([cross_re[r, 2 * q + e] * live[2 * q + e] for e in range(2)], axis=0).astype(BF16)
            ci = jnp.concatenate([cross_im[r, 2 * q + e] * live[2 * q + e] for e in range(2)], axis=0).astype(BF16)
            for k in range(4):
                lhs_ref[r, k, 16 * q : 16 * q + 16, 0:128] = cr[:, k * 128 : (k + 1) * 128]
                lhs_ref[r, k, 16 * q : 16 * q + 16, 128:256] = ci[:, k * 128 : (k + 1) * 128]
        lhs = lhs_ref[r].reshape(4 * 48, 256)
        vr = jnp.dot(lhs, ltab_ref[0], preferred_element_type=F32)
        vi = jnp.dot(lhs, ltab_ref[1], preferred_element_type=F32)
        parts = []
        for k in range(4):
            dr = vr[48 * k : 48 * (k + 1)].reshape(PAIRS, 8, 256)
            di = vi[48 * k : 48 * (k + 1)].reshape(PAIRS, 8, 256)
            c = wide_ref[16:24, 256 * k : 256 * (k + 1)][None]
            s = wide_ref[24:32, 256 * k : 256 * (k + 1)][None]
            tr, ti = dr * c - di * s, dr * s + di * c
            tr = jnp.where(sublane, tr, -tr) + pltpu.roll(tr, 4, 1)
            ti = jnp.where(sublane, ti, -ti) + pltpu.roll(ti, 4, 1)
            parts.append((tr, ti))
        r0 = parts[0][0]
        c1 = jnp.where(sublane, 1.0, ROOT_HALF)
        c3 = jnp.where(sublane, 1.0, -ROOT_HALF)
        s13 = jnp.where(sublane, 0.0, ROOT_HALF)
        r1, i1 = parts[1][0] * c1 - parts[1][1] * s13, parts[1][0] * s13 + parts[1][1] * c1
        r2 = jnp.where(sublane, parts[2][0], -parts[2][1])
        r3, i3 = parts[3][0] * c3 - parts[3][1] * s13, parts[3][0] * s13 + parts[3][1] * c3
        plus, minus, even, odd = r0 + r2, r0 - r2, r1 + r3, i1 - i3
        for m, value in enumerate((plus + even, minus - odd, plus - even, minus + odd)):
            sbuf[r][m] = value.reshape(48, 256).astype(BF16)

    row = lax.rem(chip, ROW)
    sooner = jnp.where(row < 2, 1, 0)
    later = 1 - sooner
    behind = (row == 0) | (row == ROW - 1)
    turns = [(step, j) for step in range(1, HOPS + 1) for j in order]
    for n in range(len(turns) + 1):
        if n == 8:
            for i, r in group:
                swap(i, r).start()
        if n < len(turns):
            take(turns[n][1], sooner, turns[n][0])

            @pl.when(jnp.logical_not(behind))
            def _(n=n):
                take(turns[n][1], later, turns[n][0])

        if n > 0:

            @pl.when(behind)
            def _(n=n):
                take(turns[n - 1][1], later, turns[n - 1][0])

            if turns[n - 1][0] == HOPS:
                if turns[n - 1][1] == order[0]:
                    for i, r in group:
                        swap(i, r).wait_recv()
                    for e in range(2):
                        lists(e).wait_recv()
                add_slice(turns[n - 1][1], turns[n - 1][1] == order[0])
    correlate(1, its_count)
    for i in (2, 1, 3, 0):
        back(i, 1).start()
    correlate(0, my_count)
    for i in (2, 1, 3):
        back(i, 0).start()
    land[core, cut] = sbuf[0][cut]

    for i, r in group:
        back(i, r).wait_recv()
    top = lax.broadcasted_iota(jnp.int32, (8, 256), 0) < 4
    for p in range(PAIRS):
        for y in range(2):
            halves = []
            for x in (2 * y, 2 * y + 1):
                a = land[0, x, 16 * (p // 2) : 16 * (p // 2) + 16].astype(F32)[8 * (p % 2) : 8 * (p % 2) + 8]
                b = land[1, x, 16 * (p // 2) : 16 * (p // 2) + 16].astype(F32)[8 * (p % 2) : 8 * (p % 2) + 8]
                first = jnp.where(top, a, pltpu.roll(b, 4, 0))
                second = jnp.where(top, pltpu.roll(a, 4, 0), b)
                halves.append(jnp.concatenate([first, second], axis=1))
            base = 32 * p + 16 * y
            out_ref[base : base + 16, :] = jnp.concatenate(halves, axis=0).astype(BF16)

    for n in range(2):
        lists(n).wait_send()
    for i, r in group:
        swap(i, r).wait_send()
        back(i, r).wait_send()
    for j in range(SLICES):
        for way in range(2):
            for step in range(2, HOPS + 1):
                end_hop(j, way, step)
    for way in range(2):

        @pl.when(reaches[way])
        def _(way=way):
            for i, r in whole:
                near(i, r, way).wait_send()


def shards(strain, band_taper, pair_list, pair_counts):
    narrow, wide = (jnp.asarray(t) for t in tables())
    pairs = pair_list.transpose(0, 2, 1).reshape(2, PAIRS)
    operands = (
        strain.reshape(CHAN, SAMP),
        band_taper.reshape(1, NF),
        narrow,
        wide,
        pairs,
        pair_counts,
    )
    dma = pltpu.SemaphoreType.DMA
    window = pltpu.VMEM((2 * HOPS + 1, 2, 16, 512), BF16)
    result = pltpu.VMEM((SLICES, 48, 256), BF16)
    stacks = pl.pallas_call(
        kernel,
        out_shape=jax.ShapeDtypeStruct((PAIRS * CHAN, 512), BF16),
        in_specs=[pl.BlockSpec(memory_space=pltpu.HBM)] * len(operands),
        out_specs=pl.BlockSpec(memory_space=pltpu.VMEM),
        scratch_shapes=[
            pltpu.VMEM((CHAN, SAMP), BF16),
            pltpu.VMEM((1, NF), F32),
            pltpu.VMEM((40, 1024), F32),
            pltpu.VMEM((1024, 256), BF16),
            pltpu.VMEM((2, 256, 256), BF16),
            pltpu.SMEM((2, PAIRS), jnp.int32),
            pltpu.SMEM((1,), jnp.int32),
            pltpu.SMEM((2, PAIRS), jnp.int32),
            pltpu.SMEM((1,), jnp.int32),
            pltpu.VMEM((480, 1024), BF16),
            pltpu.VMEM((480, 256), F32),
            pltpu.VMEM((2, SLICES, 16, 512), BF16),
            window,
            window,
            window,
            window,
            pltpu.VMEM((2, PAIRS, 8, 512), F32),
            pltpu.VMEM((2, PAIRS, 8, 512), F32),
            pltpu.VMEM((2, 4, 48, 256), BF16),
            result,
            result,
            pltpu.VMEM((2, SLICES, 48, 256), BF16),
            dma((9,)),
            dma((2,)),
            dma((2,)),
            dma((SLICES, 2)),
            dma((SLICES, 2)),
            dma((SLICES, 2, 2)),
            dma((SLICES, 2, 2)),
            dma((SLICES, 2, HOPS - 1)),
            dma((SLICES, 2, HOPS - 1)),
            dma((SLICES, 2)),
            dma((SLICES, 2)),
        ],
        compiler_params=pltpu.CompilerParams(
            collective_id=0, has_side_effects=True, vmem_limit_bytes=48 * 1024 * 1024
        ),
    )(*(pltpu.with_memory_space_constraint(v, pltpu.HBM) for v in operands[:-1]), pair_counts)
    return stacks.reshape(PAIRS, CHAN, 512).transpose(2, 0, 1)


def solution(mesh):
    in_specs = (P("cuts", "chan", None), P(), P("chan", None, None), P("chan"))
    out_specs = P("cuts", "chan", None)
    return jax.shard_map(shards, mesh=mesh, in_specs=in_specs, out_specs=out_specs, check_vma=False)
```

```python
import math

import jax
import jax.numpy as jnp
import ml_dtypes
import numpy as np
from jax import lax
from jax.experimental import pallas as pl
from jax.experimental.pallas import tpu as pltpu
from jax.sharding import PartitionSpec as P

SAMP = 8192
F0 = 32
NF = 960
SMOOTH = 32
PAIRS = 6
CHAN = 32
SLICES = 4
HOPS = 4
ROW = 8
SLOTS = 2 * (2 * HOPS + 1)
MESH = pl.DeviceIdType.MESH
F32 = jnp.float32
BF16 = jnp.bfloat16
ROOT_HALF = math.sqrt(0.5)


def tables():
    n2 = np.arange(1024)
    k2 = np.arange(128)
    angle = 2 * np.pi * ((n2[:, None] * k2[None, :]) % 1024) / 1024
    forward = np.concatenate([np.cos(angle), np.sin(angle)], axis=1).astype(ml_dtypes.bfloat16)
    k1 = np.arange(8)
    angle = 2 * np.pi * k1[:, None] * n2[None, :] / SAMP
    forward_turn = np.concatenate([np.cos(angle), np.sin(angle)], axis=0).astype(np.float32)
    t1 = np.arange(256)
    angle = 2 * np.pi * ((k2[:, None] * t1[None, :]) % 256) / 256
    c, s = np.cos(angle), np.sin(angle)
    lag = np.block([[c, s], [-s, c]]).astype(ml_dtypes.bfloat16)
    angle = 2 * np.pi * k1[:, None] * t1[None, :] / 2048
    gain = ((-1.0) ** k1)[:, None] / math.sqrt(NF)
    turn = np.stack([np.cos(angle) * gain, np.sin(angle) * gain])
    turn = np.repeat(turn.reshape(2, 2, 4, 1, 256), 4, axis=3)
    lag_turn = turn.transpose(0, 2, 1, 3, 4).reshape(2, 4, 8, 256).astype(np.float32)
    bins = np.arange(NF)
    count = np.minimum(bins + SMOOTH, NF - 1) - np.maximum(bins - SMOOTH, 0) + 1
    inverse = np.ones(1024)
    inverse[F0 : F0 + NF] = 1.0 / count
    inverse = inverse.reshape(128, 8).T.astype(np.float32)
    narrow = np.concatenate([forward, lag[:, :256], lag[:, 256:]], axis=0)
    wide = np.zeros((160, 1024), np.float32)
    wide[:16] = forward_turn
    wide[16:32] = lag_turn.transpose(0, 2, 1, 3).reshape(16, 1024)
    wide[32:40, :128] = inverse
    return narrow, wide


def kernel(
    x_hbm,
    taper_hbm,
    narrow_hbm,
    wide_hbm,
    pairs_hbm,
    count_hbm,
    out_ref,
    x_ref,
    taper_ref,
    wide_ref,
    ftab_ref,
    ltab_ref,
    my_pairs,
    my_count,
    its_pairs,
    its_count,
    y_ref,
    r_ref,
    stage,
    win0,
    win1,
    win2,
    win3,
    cross_re,
    cross_im,
    lhs_ref,
    sbuf0,
    sbuf1,
    land,
    load_sem,
    list_send,
    list_recv,
    swap_send,
    swap_recv,
    near_send,
    near_recv,
    hop_send,
    hop_recv,
    back_send,
    back_recv,
):
    win, sbuf = (win0, win1, win2, win3), (sbuf0, sbuf1)
    blocks = lax.axis_size("chan")
    me = lax.axis_index("chan")
    cut = lax.axis_index("cuts")
    core = lax.rem(me, 2)
    chip = me // 2
    chips = blocks // 2
    other = me + 1 - 2 * core

    def at(chan, cuts):
        return {"chan": chan, "cuts": cuts}

    def peer(i):
        return lax.rem(cut + i, SLICES)

    group = [(i, r) for i in range(SLICES) for r in range(2) if (i, r) != (0, 0)]

    def member(i, r):
        return at(other if r else me, peer(i))

    def beside(i, r, way):
        return at((other if r else me) + 2 - 4 * way, peer(i))

    barrier = pltpu.get_barrier_semaphore()
    reaches = (chip + 1 < chips, chip >= 1)
    whole = [(i, r) for i in (2, 1, 3, 0) for r in range(2)]
    for i, r in whole:
        for way in range(2):

            @pl.when(reaches[way])
            def _(i=i, r=r, way=way):
                pl.semaphore_signal(barrier, inc=1, device_id=beside(i, r, way), device_id_type=MESH)

        if (i, r) in group:
            pl.semaphore_signal(barrier, inc=1, device_id=member(i, r), device_id_type=MESH)

    loads = []
    for n, (src, dst) in enumerate(
        [
            (taper_hbm, taper_ref),
            (x_hbm.at[0:16], x_ref.at[0:16]),
            (wide_hbm.at[0:40], wide_ref),
            (x_hbm.at[16:32], x_ref.at[16:32]),
            (narrow_hbm.at[0:1024], ftab_ref),
            (pairs_hbm, my_pairs),
            (count_hbm, my_count),
            (narrow_hbm.at[1024:1280], ltab_ref.at[0]),
            (narrow_hbm.at[1280:1536], ltab_ref.at[1]),
        ]
    ):
        loads.append(pltpu.make_async_copy(src, dst, load_sem.at[n]))
    for n in range(7):
        loads[n].start()

    def taper_rows():
        row = lax.broadcasted_iota(jnp.int32, (8, NF), 0)
        bins = lax.broadcasted_iota(jnp.int32, (8, NF), 1)
        rest = jnp.where(lax.rem(bins, 8) == row, jnp.broadcast_to(taper_ref[...], (8, NF)), 0.0)
        terms = []
        for _ in range(3):
            term = rest.astype(BF16)
            rest = rest - term.astype(F32)
            terms.append(term.astype(F32))
        terms.append(jnp.zeros_like(rest))
        bins = lax.broadcasted_iota(jnp.int32, (NF, 128), 0)
        lanes = lax.broadcasted_iota(jnp.int32, (NF, 128), 1)
        pick = jnp.where(bins // 8 == lanes - F0 // 8, 1.0, 0.0).astype(BF16)
        g = jnp.dot(jnp.concatenate(terms, axis=0).astype(BF16), pick, preferred_element_type=F32)
        return g[0:8] + g[8:16] + g[16:24]

    loads[0].wait()
    taper = taper_rows()

    def put(row, o, value):
        high = value.astype(BF16)
        y_ref[row : row + 16, pl.ds(o, 128)] = high
        y_ref[480 + row : 496 + row, pl.ds(o, 128)] = (value - high.astype(F32)).astype(BF16)

    def butterflies(first, j):
        o = pl.multiple_of(j * 128, 128)
        rows = slice(first, first + 16)
        x = [x_ref[rows, pl.ds(pl.multiple_of(n1 * 1024 + o, 128), 128)].astype(F32) for n1 in range(8)]
        s = [x[n] + x[n + 4] for n in range(4)]
        d = [x[n] - x[n + 4] for n in range(4)]
        e0, e1 = s[0] + s[2], s[1] + s[3]
        dm, dp = (d[1] - d[3]) * ROOT_HALF, (d[1] + d[3]) * ROOT_HALF
        z1 = (d[0] + dm, -(d[2] + dp))
        z3 = (d[0] - dm, d[2] - dp)
        z2 = (s[0] - s[2], s[3] - s[1])
        put(first, o, e0 + e1)
        z = {1: z1, 2: z2, 3: z3, 4: (e0 - e1, None), 5: (z3[0], -z3[1]), 6: (z2[0], -z2[1]), 7: (z1[0], -z1[1])}
        for k1 in range(1, 8):
            c = wide_ref[k1 : k1 + 1, pl.ds(o, 128)]
            q = wide_ref[8 + k1 : 9 + k1, pl.ds(o, 128)]
            re, im = z[k1]
            if im is None:
                yr, yi = re * c, -(re * q)
            else:
                yr, yi = re * c + im * q, im * c - re * q
            base = 32 + 64 * (k1 - 1) + first
            put(base, o, yr)
            put(base + 32, o, yi)

    for h in range(2):
        loads[1 + 2 * h].wait()
        if h == 0:
            loads[2].wait()

        def half(j, carry, h=h):
            butterflies(16 * h, j)
            return carry

        lax.fori_loop(0, 8, half, 0)
    loads[4].wait()
    loads[7].start()
    loads[8].start()
    both = jnp.dot(y_ref[...], ftab_ref[...], preferred_element_type=F32)
    r_ref[...] = both[:480] + both[480:]

    lane = lax.broadcasted_iota(jnp.int32, (8, 128), 1)
    valid = (lane >= F0 // 8) & (lane < (F0 + NF) // 8)
    upper = lax.broadcasted_iota(jnp.int32, (8, 128), 0) < 4

    def whiten(i):
        first = pl.multiple_of(8 * peer(i), 8)
        low = r_ref[pl.ds(first, 8), :]
        re, im = [low[:, :128]], [-low[:, 128:]]
        for k1 in range(1, 8):
            a = r_ref[pl.ds(first + 64 * k1 - 32, 8), :]
            b = r_ref[pl.ds(first + 64 * k1, 8), :]
            re.append(a[:, :128] + b[:, 128:])
            im.append(b[:, :128] - a[:, 128:])
        mag = [jnp.where(valid, jnp.sqrt(re[k] * re[k] + im[k] * im[k]), 0.0) for k in range(8)]
        low = [mag[0]]
        for k in range(1, 8):
            low.append(low[-1] + mag[k])
        high = [mag[7]]
        for k in range(6, -1, -1):
            high.append(high[-1] + mag[k])
        high = high[::-1]
        total = low[7]
        middle = total
        for step in range(1, 4):
            middle = middle + pltpu.roll(total, step, 1) + pltpu.roll(total, 128 - step, 1)
        for k in range(8):
            level = (middle + pltpu.roll(high[k], 4, 1) + pltpu.roll(low[k], 124, 1)) * wide_ref[32 + k : 33 + k, 0:128]
            factor = taper[k : k + 1, :] / (level + 1e-6)
            re[k] = re[k] * factor
            im[k] = im[k] * factor
        for k in range(4):
            for h in range(2):
                rows = []
                for part in (re, im):
                    a, b = part[k], part[k + 4]
                    if h == 0:
                        rows.append(jnp.where(upper, a, pltpu.roll(b, 4, 0)))
                    else:
                        rows.append(jnp.where(upper, pltpu.roll(a, 4, 0), b))
                stage[h, i, :, k * 128 : (k + 1) * 128] = jnp.concatenate(rows, axis=0).astype(BF16)

    def swap(i, r):
        return pltpu.make_async_remote_copy(
            src_ref=stage.at[1 - core if r else core, i],
            dst_ref=win[(SLICES - i) % SLICES].at[HOPS, core],
            send_sem=swap_send.at[i, r],
            recv_sem=swap_recv.at[i, r],
            device_id=member(i, r),
            device_id_type=MESH,
        )

    def near(i, r, way):
        return pltpu.make_async_remote_copy(
            src_ref=stage.at[1 - core if r else core, i],
            dst_ref=win[(SLICES - i) % SLICES].at[HOPS + 2 * way - 1, core],
            send_sem=near_send.at[i, r, way],
            recv_sem=near_recv.at[i, r, way],
            device_id=beside(i, r, way),
            device_id_type=MESH,
        )

    def hop(j, way, step):
        sign = 2 * way - 1
        return pltpu.make_async_remote_copy(
            src_ref=win[j].at[HOPS + sign * (step - 1)],
            dst_ref=win[j].at[HOPS + sign * step],
            send_sem=hop_send.at[j, way, step - 2],
            recv_sem=hop_recv.at[j, way, step - 2],
            device_id=at(me - 2 * sign, cut),
            device_id_type=MESH,
        )

    def comes(way, step):
        return jnp.where(way == 0, chip, chips - 1 - chip) >= step

    def goes(way, step):
        return comes(way, step - 1) & (jnp.where(way == 0, chips - 1 - chip, chip) >= 1)

    def end_hop(j, way, step):
        @pl.when(goes(way, step))
        def _():
            hop(j, way, step).wait_send()

    def take(j, way, step):
        @pl.when(comes(way, step))
        def _():
            if step == 1:
                for r in range(2):
                    near((SLICES - j) % SLICES, r, way).wait_recv()
            else:
                hop(j, way, step).wait_recv()

        if step < HOPS:

            @pl.when(goes(way, step + 1))
            def _():
                hop(j, way, step + 1).start()

    def back(i, r):
        return pltpu.make_async_remote_copy(
            src_ref=sbuf[r].at[peer(i)],
            dst_ref=land.at[core, cut],
            send_sem=back_send.at[i, r],
            recv_sem=back_recv.at[i, r],
            device_id=member(i, r),
            device_id_type=MESH,
        )

    def lists(n):
        src, dst = ((pairs_hbm, its_pairs), (count_hbm, its_count))[n]
        return pltpu.make_async_remote_copy(
            src_ref=src,
            dst_ref=dst,
            send_sem=list_send.at[n],
            recv_sem=list_recv.at[n],
            device_id=at(other, cut),
            device_id_type=MESH,
        )

    order = (0, 1, 3, 2)
    for n, i in enumerate((0, 3, 1, 2)):
        whiten(i)
        if n == 0:
            pl.semaphore_wait(barrier, 7 + jnp.where(reaches[0], 8, 0) + jnp.where(reaches[1], 8, 0))
        for way in range(2):

            @pl.when(reaches[way])
            def _(way=way, i=i):
                for r in range(2):
                    near(i, r, way).start()

    win[0][HOPS, core] = stage[core, 0]
    for n in range(2):
        lists(n).start()
    for n in (5, 6, 7, 8):
        loads[n].wait()

    def add_slice(j, fresh):
        first = me - core

        def pair(p, carry):
            for r, pairs in ((0, my_pairs), (1, its_pairs)):
                a_slot = jnp.clip(pairs[0, p] - first + 2 * HOPS, 0, SLOTS - 1)
                b_slot = jnp.clip(pairs[1, p] - first + 2 * HOPS, 0, SLOTS - 1)
                a = win[j][a_slot // 2, lax.rem(a_slot, 2)].astype(F32)
                b = win[j][b_slot // 2, lax.rem(b_slot, 2)].astype(F32)
                ar, ai, br, bi = a[:8], a[8:], b[:8], b[8:]
                tr, ti = ar * br + ai * bi, ai * br - ar * bi
                if not fresh:
                    tr, ti = tr + cross_re[r, p], ti + cross_im[r, p]
                cross_re[r, p] = tr
                cross_im[r, p] = ti
            return carry

        lax.fori_loop(0, PAIRS, pair, 0)

    sublane = lax.broadcasted_iota(jnp.int32, (1, 8, 1), 1) < 4

    def correlate(r, count_ref):
        live = [jnp.where(p < count_ref[0], 1.0, 0.0).astype(F32) for p in range(PAIRS)]
        for q in range(PAIRS // 2):
            cr = jnp.concatenate([cross_re[r, 2 * q + e] * live[2 * q + e] for e in range(2)], axis=0).astype(BF16)
            ci = jnp.concatenate([cross_im[r, 2 * q + e] * live[2 * q + e] for e in range(2)], axis=0).astype(BF16)
            for k in range(4):
                lhs_ref[r, k, 16 * q : 16 * q + 16, 0:128] = cr[:, k * 128 : (k + 1) * 128]
                lhs_ref[r, k, 16 * q : 16 * q + 16, 128:256] = ci[:, k * 128 : (k + 1) * 128]
        lhs = lhs_ref[r].reshape(4 * 48, 256)
        vr = jnp.dot(lhs, ltab_ref[0], preferred_element_type=F32)
        vi = jnp.dot(lhs, ltab_ref[1], preferred_element_type=F32)
        parts = []
        for k in range(4):
            dr = vr[48 * k : 48 * (k + 1)].reshape(PAIRS, 8, 256)
            di = vi[48 * k : 48 * (k + 1)].reshape(PAIRS, 8, 256)
            c = wide_ref[16:24, 256 * k : 256 * (k + 1)][None]
            s = wide_ref[24:32, 256 * k : 256 * (k + 1)][None]
            tr, ti = dr * c - di * s, dr * s + di * c
            tr = jnp.where(sublane, tr, -tr) + pltpu.roll(tr, 4, 1)
            ti = jnp.where(sublane, ti, -ti) + pltpu.roll(ti, 4, 1)
            parts.append((tr, ti))
        r0 = parts[0][0]
        c1 = jnp.where(sublane, 1.0, ROOT_HALF)
        c3 = jnp.where(sublane, 1.0, -ROOT_HALF)
        s13 = jnp.where(sublane, 0.0, ROOT_HALF)
        r1, i1 = parts[1][0] * c1 - parts[1][1] * s13, parts[1][0] * s13 + parts[1][1] * c1
        r2 = jnp.where(sublane, parts[2][0], -parts[2][1])
        r3, i3 = parts[3][0] * c3 - parts[3][1] * s13, parts[3][0] * s13 + parts[3][1] * c3
        plus, minus, even, odd = r0 + r2, r0 - r2, r1 + r3, i1 - i3
        for m, value in enumerate((plus + even, minus - odd, plus - even, minus + odd)):
            sbuf[r][m] = value.reshape(48, 256).astype(BF16)

    row = lax.rem(chip, ROW)
    sooner = jnp.where(row < 2, 1, 0)
    later = 1 - sooner
    behind = (row == 0) | (row == ROW - 1)
    turns = [(step, j) for step in range(1, HOPS + 1) for j in order]
    for n in range(len(turns) + 1):
        if n == 8:
            for i, r in group:
                swap(i, r).start()
        if n < len(turns):
            take(turns[n][1], sooner, turns[n][0])

            @pl.when(jnp.logical_not(behind))
            def _(n=n):
                take(turns[n][1], later, turns[n][0])

        if n > 0:

            @pl.when(behind)
            def _(n=n):
                take(turns[n - 1][1], later, turns[n - 1][0])

            if turns[n - 1][0] == HOPS:
                if turns[n - 1][1] == order[0]:
                    for i, r in group:
                        swap(i, r).wait_recv()
                    for e in range(2):
                        lists(e).wait_recv()
                add_slice(turns[n - 1][1], turns[n - 1][1] == order[0])
    correlate(1, its_count)
    for i in (2, 1, 3, 0):
        back(i, 1).start()
    correlate(0, my_count)
    for i in (2, 1, 3):
        back(i, 0).start()
    land[core, cut] = sbuf[0][cut]

    for i, r in group:
        back(i, r).wait_recv()
    top = lax.broadcasted_iota(jnp.int32, (8, 256), 0) < 4
    for p in range(PAIRS):
        for y in range(2):
            halves = []
            for x in (2 * y, 2 * y + 1):
                a = land[0, x, 16 * (p // 2) : 16 * (p // 2) + 16].astype(F32)[8 * (p % 2) : 8 * (p % 2) + 8]
                b = land[1, x, 16 * (p // 2) : 16 * (p // 2) + 16].astype(F32)[8 * (p % 2) : 8 * (p % 2) + 8]
                first = jnp.where(top, a, pltpu.roll(b, 4, 0))
                second = jnp.where(top, pltpu.roll(a, 4, 0), b)
                halves.append(jnp.concatenate([first, second], axis=1))
            base = 32 * p + 16 * y
            out_ref[base : base + 16, :] = jnp.concatenate(halves, axis=0).astype(BF16)

    for n in range(2):
        lists(n).wait_send()
    for i, r in group:
        swap(i, r).wait_send()
        back(i, r).wait_send()
    for j in range(SLICES):
        for way in range(2):
            for step in range(2, HOPS + 1):
                end_hop(j, way, step)
    for way in range(2):

        @pl.when(reaches[way])
        def _(way=way):
            for i, r in whole:
                near(i, r, way).wait_send()


def shards(strain, band_taper, pair_list, pair_counts):
    narrow, wide = (jnp.asarray(t) for t in tables())
    pairs = pair_list.transpose(0, 2, 1).reshape(2, PAIRS)
    operands = (
        strain.reshape(CHAN, SAMP),
        band_taper.reshape(1, NF),
        narrow,
        wide,
        pairs,
        pair_counts,
    )
    dma = pltpu.SemaphoreType.DMA
    window = pltpu.VMEM((2 * HOPS + 1, 2, 16, 512), BF16)
    result = pltpu.VMEM((SLICES, 48, 256), BF16)
    stacks = pl.pallas_call(
        kernel,
        out_shape=jax.ShapeDtypeStruct((PAIRS * CHAN, 512), BF16),
        in_specs=[pl.BlockSpec(memory_space=pltpu.HBM)] * len(operands),
        out_specs=pl.BlockSpec(memory_space=pltpu.VMEM),
        scratch_shapes=[
            pltpu.VMEM((CHAN, SAMP), BF16),
            pltpu.VMEM((1, NF), F32),
            pltpu.VMEM((40, 1024), F32),
            pltpu.VMEM((1024, 256), BF16),
            pltpu.VMEM((2, 256, 256), BF16),
            pltpu.SMEM((2, PAIRS), jnp.int32),
            pltpu.SMEM((1,), jnp.int32),
            pltpu.SMEM((2, PAIRS), jnp.int32),
            pltpu.SMEM((1,), jnp.int32),
            pltpu.VMEM((960, 1024), BF16),
            pltpu.VMEM((480, 256), F32),
            pltpu.VMEM((2, SLICES, 16, 512), BF16),
            window,
            window,
            window,
            window,
            pltpu.VMEM((2, PAIRS, 8, 512), F32),
            pltpu.VMEM((2, PAIRS, 8, 512), F32),
            pltpu.VMEM((2, 4, 48, 256), BF16),
            result,
            result,
            pltpu.VMEM((2, SLICES, 48, 256), BF16),
            dma((9,)),
            dma((2,)),
            dma((2,)),
            dma((SLICES, 2)),
            dma((SLICES, 2)),
            dma((SLICES, 2, 2)),
            dma((SLICES, 2, 2)),
            dma((SLICES, 2, HOPS - 1)),
            dma((SLICES, 2, HOPS - 1)),
            dma((SLICES, 2)),
            dma((SLICES, 2)),
        ],
        compiler_params=pltpu.CompilerParams(
            collective_id=0, has_side_effects=True, vmem_limit_bytes=48 * 1024 * 1024
        ),
    )(*(pltpu.with_memory_space_constraint(v, pltpu.HBM) for v in operands[:-1]), pair_counts)
    return stacks.reshape(PAIRS, CHAN, 512).transpose(2, 0, 1)


def solution(mesh):
    in_specs = (P("cuts", "chan", None), P(), P("chan", None, None), P("chan"))
    out_specs = P("cuts", "chan", None)
    return jax.shard_map(shards, mesh=mesh, in_specs=in_specs, out_specs=out_specs, check_vma=False)
```

```python
import math

import jax
import jax.numpy as jnp
import ml_dtypes
import numpy as np
from jax import lax
from jax.experimental import pallas as pl
from jax.experimental.pallas import tpu as pltpu
from jax.sharding import PartitionSpec as P

SAMP = 8192
F0 = 32
NF = 960
SMOOTH = 32
PAIRS = 6
CHAN = 32
SLICES = 4
HOPS = 4
ROW = 8
SLOTS = 2 * (2 * HOPS + 1)
MESH = pl.DeviceIdType.MESH
F32 = jnp.float32
BF16 = jnp.bfloat16
ROOT_HALF = math.sqrt(0.5)


def tables():
    n2 = np.arange(1024)
    k2 = np.arange(128)
    angle = 2 * np.pi * ((n2[:, None] * k2[None, :]) % 1024) / 1024
    forward = np.concatenate([np.cos(angle), np.sin(angle)], axis=1).astype(ml_dtypes.bfloat16)
    k1 = np.arange(8)
    angle = 2 * np.pi * k1[:, None] * n2[None, :] / SAMP
    forward_turn = np.concatenate([np.cos(angle), np.sin(angle)], axis=0).astype(np.float32)
    t1 = np.arange(256)
    angle = 2 * np.pi * ((k2[:, None] * t1[None, :]) % 256) / 256
    c, s = np.cos(angle), np.sin(angle)
    lag = np.block([[c, s], [-s, c]]).astype(ml_dtypes.bfloat16)
    angle = 2 * np.pi * k1[:, None] * t1[None, :] / 2048
    gain = ((-1.0) ** k1)[:, None] / math.sqrt(NF)
    turn = np.stack([np.cos(angle) * gain, np.sin(angle) * gain])
    turn = np.repeat(turn.reshape(2, 2, 4, 1, 256), 4, axis=3)
    lag_turn = turn.transpose(0, 2, 1, 3, 4).reshape(2, 4, 8, 256).astype(np.float32)
    bins = np.arange(NF)
    count = np.minimum(bins + SMOOTH, NF - 1) - np.maximum(bins - SMOOTH, 0) + 1
    inverse = np.ones(1024)
    inverse[F0 : F0 + NF] = 1.0 / count
    inverse = inverse.reshape(128, 8).T.astype(np.float32)
    narrow = np.concatenate([forward, lag[:, :256], lag[:, 256:]], axis=0)
    wide = np.zeros((160, 1024), np.float32)
    wide[:16] = forward_turn
    wide[16:32] = lag_turn.transpose(0, 2, 1, 3).reshape(16, 1024)
    wide[32:40, :128] = inverse
    return narrow, wide


def kernel(
    x_hbm,
    taper_hbm,
    narrow_hbm,
    wide_hbm,
    pairs_hbm,
    count_hbm,
    out_ref,
    x_ref,
    taper_ref,
    wide_ref,
    ftab_ref,
    ltab_ref,
    my_pairs,
    my_count,
    its_pairs,
    its_count,
    y_ref,
    r_ref,
    stage,
    win0,
    win1,
    win2,
    win3,
    cross_re,
    cross_im,
    lhs_ref,
    sbuf0,
    sbuf1,
    land,
    load_sem,
    list_send,
    list_recv,
    swap_send,
    swap_recv,
    near_send,
    near_recv,
    hop_send,
    hop_recv,
    back_send,
    back_recv,
):
    win, sbuf = (win0, win1, win2, win3), (sbuf0, sbuf1)
    blocks = lax.axis_size("chan")
    me = lax.axis_index("chan")
    cut = lax.axis_index("cuts")
    core = lax.rem(me, 2)
    chip = me // 2
    chips = blocks // 2
    other = me + 1 - 2 * core

    def at(chan, cuts):
        return {"chan": chan, "cuts": cuts}

    def peer(i):
        return lax.rem(cut + i, SLICES)

    group = [(i, r) for i in range(SLICES) for r in range(2) if (i, r) != (0, 0)]

    def member(i, r):
        return at(other if r else me, peer(i))

    def beside(i, r, way):
        return at((other if r else me) + 2 - 4 * way, peer(i))

    barrier = pltpu.get_barrier_semaphore()
    reaches = (chip + 1 < chips, chip >= 1)
    whole = [(i, r) for i in (2, 1, 3, 0) for r in range(2)]
    for i, r in whole:
        for way in range(2):

            @pl.when(reaches[way])
            def _(i=i, r=r, way=way):
                pl.semaphore_signal(barrier, inc=1, device_id=beside(i, r, way), device_id_type=MESH)

        if (i, r) in group:
            pl.semaphore_signal(barrier, inc=1, device_id=member(i, r), device_id_type=MESH)

    loads = []
    for n, (src, dst) in enumerate(
        [
            (taper_hbm, taper_ref),
            (x_hbm.at[0:16], x_ref.at[0:16]),
            (wide_hbm.at[0:40], wide_ref),
            (x_hbm.at[16:32], x_ref.at[16:32]),
            (narrow_hbm.at[0:1024], ftab_ref),
            (pairs_hbm, my_pairs),
            (count_hbm, my_count),
            (narrow_hbm.at[1024:1280], ltab_ref.at[0]),
            (narrow_hbm.at[1280:1536], ltab_ref.at[1]),
        ]
    ):
        loads.append(pltpu.make_async_copy(src, dst, load_sem.at[n]))
    for n in range(7):
        loads[n].start()

    def taper_rows():
        row = lax.broadcasted_iota(jnp.int32, (8, NF), 0)
        bins = lax.broadcasted_iota(jnp.int32, (8, NF), 1)
        rest = jnp.where(lax.rem(bins, 8) == row, jnp.broadcast_to(taper_ref[...], (8, NF)), 0.0)
        terms = []
        for _ in range(3):
            term = rest.astype(BF16)
            rest = rest - term.astype(F32)
            terms.append(term.astype(F32))
        terms.append(jnp.zeros_like(rest))
        bins = lax.broadcasted_iota(jnp.int32, (NF, 128), 0)
        lanes = lax.broadcasted_iota(jnp.int32, (NF, 128), 1)
        pick = jnp.where(bins // 8 == lanes - F0 // 8, 1.0, 0.0).astype(BF16)
        g = jnp.dot(jnp.concatenate(terms, axis=0).astype(BF16), pick, preferred_element_type=F32)
        return g[0:8] + g[8:16] + g[16:24]

    loads[0].wait()
    taper = taper_rows()

    def put(row, o, value):
        high = value.astype(BF16)
        y_ref[row : row + 16, pl.ds(o, 128)] = high
        y_ref[480 + row : 496 + row, pl.ds(o, 128)] = (value - high.astype(F32)).astype(BF16)

    def butterflies(first, j):
        o = pl.multiple_of(j * 128, 128)
        rows = slice(first, first + 16)
        x = [x_ref[rows, pl.ds(pl.multiple_of(n1 * 1024 + o, 128), 128)].astype(F32) for n1 in range(8)]
        s = [x[n] + x[n + 4] for n in range(4)]
        d = [x[n] - x[n + 4] for n in range(4)]
        e0, e1 = s[0] + s[2], s[1] + s[3]
        dm, dp = (d[1] - d[3]) * ROOT_HALF, (d[1] + d[3]) * ROOT_HALF
        z1 = (d[0] + dm, -(d[2] + dp))
        z3 = (d[0] - dm, d[2] - dp)
        z2 = (s[0] - s[2], s[3] - s[1])
        put(first, o, e0 + e1)
        z = {1: z1, 2: z2, 3: z3, 4: (e0 - e1, None), 5: (z3[0], -z3[1]), 6: (z2[0], -z2[1]), 7: (z1[0], -z1[1])}
        for k1 in range(1, 8):
            c = wide_ref[k1 : k1 + 1, pl.ds(o, 128)]
            q = wide_ref[8 + k1 : 9 + k1, pl.ds(o, 128)]
            re, im = z[k1]
            if im is None:
                yr, yi = re * c, -(re * q)
            else:
                yr, yi = re * c + im * q, im * c - re * q
            base = 32 + 64 * (k1 - 1) + first
            put(base, o, yr)
            put(base + 32, o, yi)

    for h in range(2):
        loads[1 + 2 * h].wait()
        if h == 0:
            loads[2].wait()

        def half(j, carry, h=h):
            butterflies(16 * h, j)
            return carry

        lax.fori_loop(0, 8, half, 0)
    loads[4].wait()
    loads[7].start()
    loads[8].start()
    both = jnp.dot(y_ref[...], ftab_ref[...], preferred_element_type=F32)
    r_ref[...] = both[:480] + both[480:]

    lane = lax.broadcasted_iota(jnp.int32, (8, 128), 1)
    valid = (lane >= F0 // 8) & (lane < (F0 + NF) // 8)
    upper = lax.broadcasted_iota(jnp.int32, (8, 128), 0) < 4

    def whiten(i):
        first = pl.multiple_of(8 * peer(i), 8)
        low = r_ref[pl.ds(first, 8), :]
        re, im = [low[:, :128]], [-low[:, 128:]]
        for k1 in range(1, 8):
            a = r_ref[pl.ds(first + 64 * k1 - 32, 8), :]
            b = r_ref[pl.ds(first + 64 * k1, 8), :]
            re.append(a[:, :128] + b[:, 128:])
            im.append(b[:, :128] - a[:, 128:])
        mag = [jnp.where(valid, jnp.sqrt(re[k] * re[k] + im[k] * im[k]), 0.0) for k in range(8)]
        low = [mag[0]]
        for k in range(1, 8):
            low.append(low[-1] + mag[k])
        high = [mag[7]]
        for k in range(6, -1, -1):
            high.append(high[-1] + mag[k])
        high = high[::-1]
        total = low[7]
        middle = total
        for step in range(1, 4):
            middle = middle + pltpu.roll(total, step, 1) + pltpu.roll(total, 128 - step, 1)
        for k in range(8):
            level = (middle + pltpu.roll(high[k], 4, 1) + pltpu.roll(low[k], 124, 1)) * wide_ref[32 + k : 33 + k, 0:128]
            factor = taper[k : k + 1, :] / (level + 1e-6)
            re[k] = re[k] * factor
            im[k] = im[k] * factor
        for k in range(4):
            for h in range(2):
                rows = []
                for part in (re, im):
                    a, b = part[k], part[k + 4]
                    if h == 0:
                        rows.append(jnp.where(upper, a, pltpu.roll(b, 4, 0)))
                    else:
                        rows.append(jnp.where(upper, pltpu.roll(a, 4, 0), b))
                stage[h, i, :, k * 128 : (k + 1) * 128] = jnp.concatenate(rows, axis=0).astype(BF16)

    def swap(i, r):
        return pltpu.make_async_remote_copy(
            src_ref=stage.at[1 - core if r else core, i],
            dst_ref=win[(SLICES - i) % SLICES].at[HOPS, core],
            send_sem=swap_send.at[i, r],
            recv_sem=swap_recv.at[i, r],
            device_id=member(i, r),
            device_id_type=MESH,
        )

    def near(i, r, way):
        return pltpu.make_async_remote_copy(
            src_ref=stage.at[1 - core if r else core, i],
            dst_ref=win[(SLICES - i) % SLICES].at[HOPS + 2 * way - 1, core],
            send_sem=near_send.at[i, r, way],
            recv_sem=near_recv.at[i, r, way],
            device_id=beside(i, r, way),
            device_id_type=MESH,
        )

    def hop(j, way, step):
        sign = 2 * way - 1
        return pltpu.make_async_remote_copy(
            src_ref=win[j].at[HOPS + sign * (step - 1)],
            dst_ref=win[j].at[HOPS + sign * step],
            send_sem=hop_send.at[j, way, step - 2],
            recv_sem=hop_recv.at[j, way, step - 2],
            device_id=at(me - 2 * sign, cut),
            device_id_type=MESH,
        )

    def comes(way, step):
        return jnp.where(way == 0, chip, chips - 1 - chip) >= step

    def goes(way, step):
        return comes(way, step - 1) & (jnp.where(way == 0, chips - 1 - chip, chip) >= 1)

    def end_hop(j, way, step):
        @pl.when(goes(way, step))
        def _():
            hop(j, way, step).wait_send()

    def take(j, way, step):
        @pl.when(comes(way, step))
        def _():
            if step == 1:
                for r in range(2):
                    near((SLICES - j) % SLICES, r, way).wait_recv()
            else:
                hop(j, way, step).wait_recv()

        if step < HOPS:

            @pl.when(goes(way, step + 1))
            def _():
                hop(j, way, step + 1).start()

    def back(i, r):
        return pltpu.make_async_remote_copy(
            src_ref=sbuf[r].at[peer(i)],
            dst_ref=land.at[core, cut],
            send_sem=back_send.at[i, r],
            recv_sem=back_recv.at[i, r],
            device_id=member(i, r),
            device_id_type=MESH,
        )

    def lists(n):
        src, dst = ((pairs_hbm, its_pairs), (count_hbm, its_count))[n]
        return pltpu.make_async_remote_copy(
            src_ref=src,
            dst_ref=dst,
            send_sem=list_send.at[n],
            recv_sem=list_recv.at[n],
            device_id=at(other, cut),
            device_id_type=MESH,
        )

    order = (0, 1, 3, 2)
    for n, i in enumerate((0, 3, 1, 2)):
        whiten(i)
        if n == 0:
            pl.semaphore_wait(barrier, 7 + jnp.where(reaches[0], 8, 0) + jnp.where(reaches[1], 8, 0))
        for way in range(2):

            @pl.when(reaches[way])
            def _(way=way, i=i):
                for r in range(2):
                    near(i, r, way).start()

    win[0][HOPS, core] = stage[core, 0]
    for n in range(2):
        lists(n).start()
    for n in (5, 6, 7, 8):
        loads[n].wait()

    def add_slice(j, fresh):
        first = me - core

        def pair(p, carry):
            for r, pairs in ((0, my_pairs), (1, its_pairs)):
                a_slot = jnp.clip(pairs[0, p] - first + 2 * HOPS, 0, SLOTS - 1)
                b_slot = jnp.clip(pairs[1, p] - first + 2 * HOPS, 0, SLOTS - 1)
                a = win[j][a_slot // 2, lax.rem(a_slot, 2)].astype(F32)
                b = win[j][b_slot // 2, lax.rem(b_slot, 2)].astype(F32)
                ar, ai, br, bi = a[:8], a[8:], b[:8], b[8:]
                tr, ti = ar * br + ai * bi, ai * br - ar * bi
                if not fresh:
                    tr, ti = tr + cross_re[r, p], ti + cross_im[r, p]
                cross_re[r, p] = tr
                cross_im[r, p] = ti
            return carry

        lax.fori_loop(0, PAIRS, pair, 0)

    sublane = lax.broadcasted_iota(jnp.int32, (1, 8, 1), 1) < 4

    def correlate(r, count_ref):
        live = [jnp.where(p < count_ref[0], 1.0, 0.0).astype(F32) for p in range(PAIRS)]
        for q in range(PAIRS // 2):
            cr = jnp.concatenate([cross_re[r, 2 * q + e] * live[2 * q + e] for e in range(2)], axis=0).astype(BF16)
            ci = jnp.concatenate([cross_im[r, 2 * q + e] * live[2 * q + e] for e in range(2)], axis=0).astype(BF16)
            for k in range(4):
                lhs_ref[r, k, 16 * q : 16 * q + 16, 0:128] = cr[:, k * 128 : (k + 1) * 128]
                lhs_ref[r, k, 16 * q : 16 * q + 16, 128:256] = ci[:, k * 128 : (k + 1) * 128]
        lhs = lhs_ref[r].reshape(4 * 48, 256)
        vr = jnp.dot(lhs, ltab_ref[0], preferred_element_type=F32)
        vi = jnp.dot(lhs, ltab_ref[1], preferred_element_type=F32)
        parts = []
        for k in range(4):
            dr = vr[48 * k : 48 * (k + 1)].reshape(PAIRS, 8, 256)
            di = vi[48 * k : 48 * (k + 1)].reshape(PAIRS, 8, 256)
            c = wide_ref[16:24, 256 * k : 256 * (k + 1)][None]
            s = wide_ref[24:32, 256 * k : 256 * (k + 1)][None]
            tr, ti = dr * c - di * s, dr * s + di * c
            tr = jnp.where(sublane, tr, -tr) + pltpu.roll(tr, 4, 1)
            ti = jnp.where(sublane, ti, -ti) + pltpu.roll(ti, 4, 1)
            parts.append((tr, ti))
        r0 = parts[0][0]
        c1 = jnp.where(sublane, 1.0, ROOT_HALF)
        c3 = jnp.where(sublane, 1.0, -ROOT_HALF)
        s13 = jnp.where(sublane, 0.0, ROOT_HALF)
        r1, i1 = parts[1][0] * c1 - parts[1][1] * s13, parts[1][0] * s13 + parts[1][1] * c1
        r2 = jnp.where(sublane, parts[2][0], -parts[2][1])
        r3, i3 = parts[3][0] * c3 - parts[3][1] * s13, parts[3][0] * s13 + parts[3][1] * c3
        plus, minus, even, odd = r0 + r2, r0 - r2, r1 + r3, i1 - i3
        for m, value in enumerate((plus + even, minus - odd, plus - even, minus + odd)):
            sbuf[r][m] = value.reshape(48, 256).astype(BF16)

    row = lax.rem(chip, ROW)
    sooner = jnp.where(row < 2, 1, 0)
    later = 1 - sooner
    behind = (row == 0) | (row == ROW - 1)
    turns = [(step, j) for step in range(1, HOPS + 1) for j in order]
    for n in range(len(turns) + 1):
        if n == 8:
            for i, r in group:
                swap(i, r).start()
        if n < len(turns):
            take(turns[n][1], sooner, turns[n][0])

            @pl.when(jnp.logical_not(behind))
            def _(n=n):
                take(turns[n][1], later, turns[n][0])

        if n > 0:

            @pl.when(behind)
            def _(n=n):
                take(turns[n - 1][1], later, turns[n - 1][0])

            if turns[n - 1][0] == HOPS:
                if turns[n - 1][1] == order[0]:
                    for i, r in group:
                        swap(i, r).wait_recv()
                    for e in range(2):
                        lists(e).wait_recv()
                add_slice(turns[n - 1][1], turns[n - 1][1] == order[0])
    correlate(1, its_count)
    back(2, 1).start()
    correlate(0, my_count)
    back(2, 0).start()
    for i, r in ((3, 1), (1, 1), (3, 0), (1, 0), (0, 1)):
        back(i, r).start()
    land[core, cut] = sbuf[0][cut]

    for i, r in group:
        back(i, r).wait_recv()
    top = lax.broadcasted_iota(jnp.int32, (8, 256), 0) < 4
    for p in range(PAIRS):
        for y in range(2):
            halves = []
            for x in (2 * y, 2 * y + 1):
                a = land[0, x, 16 * (p // 2) : 16 * (p // 2) + 16].astype(F32)[8 * (p % 2) : 8 * (p % 2) + 8]
                b = land[1, x, 16 * (p // 2) : 16 * (p // 2) + 16].astype(F32)[8 * (p % 2) : 8 * (p % 2) + 8]
                first = jnp.where(top, a, pltpu.roll(b, 4, 0))
                second = jnp.where(top, pltpu.roll(a, 4, 0), b)
                halves.append(jnp.concatenate([first, second], axis=1))
            base = 32 * p + 16 * y
            out_ref[base : base + 16, :] = jnp.concatenate(halves, axis=0).astype(BF16)

    for n in range(2):
        lists(n).wait_send()
    for i, r in group:
        swap(i, r).wait_send()
        back(i, r).wait_send()
    for j in range(SLICES):
        for way in range(2):
            for step in range(2, HOPS + 1):
                end_hop(j, way, step)
    for way in range(2):

        @pl.when(reaches[way])
        def _(way=way):
            for i, r in whole:
                near(i, r, way).wait_send()


def shards(strain, band_taper, pair_list, pair_counts):
    narrow, wide = (jnp.asarray(t) for t in tables())
    pairs = pair_list.transpose(0, 2, 1).reshape(2, PAIRS)
    operands = (
        strain.reshape(CHAN, SAMP),
        band_taper.reshape(1, NF),
        narrow,
        wide,
        pairs,
        pair_counts,
    )
    dma = pltpu.SemaphoreType.DMA
    window = pltpu.VMEM((2 * HOPS + 1, 2, 16, 512), BF16)
    result = pltpu.VMEM((SLICES, 48, 256), BF16)
    stacks = pl.pallas_call(
        kernel,
        out_shape=jax.ShapeDtypeStruct((PAIRS * CHAN, 512), BF16),
        in_specs=[pl.BlockSpec(memory_space=pltpu.HBM)] * len(operands),
        out_specs=pl.BlockSpec(memory_space=pltpu.VMEM),
        scratch_shapes=[
            pltpu.VMEM((CHAN, SAMP), BF16),
            pltpu.VMEM((1, NF), F32),
            pltpu.VMEM((40, 1024), F32),
            pltpu.VMEM((1024, 256), BF16),
            pltpu.VMEM((2, 256, 256), BF16),
            pltpu.SMEM((2, PAIRS), jnp.int32),
            pltpu.SMEM((1,), jnp.int32),
            pltpu.SMEM((2, PAIRS), jnp.int32),
            pltpu.SMEM((1,), jnp.int32),
            pltpu.VMEM((960, 1024), BF16),
            pltpu.VMEM((480, 256), F32),
            pltpu.VMEM((2, SLICES, 16, 512), BF16),
            window,
            window,
            window,
            window,
            pltpu.VMEM((2, PAIRS, 8, 512), F32),
            pltpu.VMEM((2, PAIRS, 8, 512), F32),
            pltpu.VMEM((2, 4, 48, 256), BF16),
            result,
            result,
            pltpu.VMEM((2, SLICES, 48, 256), BF16),
            dma((9,)),
            dma((2,)),
            dma((2,)),
            dma((SLICES, 2)),
            dma((SLICES, 2)),
            dma((SLICES, 2, 2)),
            dma((SLICES, 2, 2)),
            dma((SLICES, 2, HOPS - 1)),
            dma((SLICES, 2, HOPS - 1)),
            dma((SLICES, 2)),
            dma((SLICES, 2)),
        ],
        compiler_params=pltpu.CompilerParams(
            collective_id=0, has_side_effects=True, vmem_limit_bytes=48 * 1024 * 1024
        ),
    )(*(pltpu.with_memory_space_constraint(v, pltpu.HBM) for v in operands[:-1]), pair_counts)
    return stacks.reshape(PAIRS, CHAN, 512).transpose(2, 0, 1)


def solution(mesh):
    in_specs = (P("cuts", "chan", None), P(), P("chan", None, None), P("chan"))
    out_specs = P("cuts", "chan", None)
    return jax.shard_map(shards, mesh=mesh, in_specs=in_specs, out_specs=out_specs, check_vma=False)
```
